256 devices in a mesh: gx: 16 (over z_hi, x), gy: 4 (over y), gz: 4 (over z_lo, core).
Axes of the slice: x: 4, y: 4, z: 8 (z_hi: 4, z_lo: 2; z = z_hi * 2 + z_lo), core: 2. Of those that a mesh axis runs over, the one named last changes fastest.
Arguments:
- fluid_populations: float32 [19, 64, 64, 512], P(None, 'gx', 'gy', 'gz'), may hold values from 0 to 10, as said below
- order_populations: float32 [19, 64, 64, 512], P(None, 'gx', 'gy', 'gz'), may hold values from -0.5 to 0.5
- plane_offsets: int32 [2, 4], replicated, may hold values from 0 to 63
- plane_weights: float32 [4], replicated, may hold values from 0.1 to 0.9
Outputs:
- fluid_next: float32 [19, 64, 64, 512], P(None, 'gx', 'gy', 'gz')
- order_next: float32 [19, 64, 64, 512], P(None, 'gx', 'gy', 'gz')
The draws below stay inside these ranges and needn't reach their ends.
Inputs may be any that keep to these rules, and one draw needn't show every extreme that they name: `fluid_populations`: every entry is positive.
All inputs are finite; a program needn't handle non-finite values.
Results may differ from the reference program's by a relative error of at most 0.0001.
Values sent between devices are 32-bit elements; how exact they have to be, the bound alone decides.
No kernel may reach another device: no remote copies, remote signals or barrier semaphores. Data moves between devices by JAX's collectives and lax.ppermute only.
A program may use at most 128 MiB of HBM per device.

```python
import math
import jax
import jax.numpy as jnp
from jax import lax

CY = 16
STEPS = 2
NX = 64
NY = 64
NZ = 512
N_GY = 4


def lattice_table():
    return jnp.array([1.0 / 3.0] + [1.0 / 18.0] * 6 + [1.0 / 36.0] * 12, jnp.float32).reshape(19, 1, 1, 1)


def draw_fluid_populations(key, part):
    key = jax.random.fold_in(key, 11)
    first_key, second_key = jax.random.split(key)
    density = jnp.exp(jax.random.uniform(first_key, (1, NX, NY, NZ), jnp.float32, math.log(2.0), math.log(20.0)))
    spread = jax.random.uniform(second_key, (19, NX, NY, NZ), jnp.float32, -0.4, 0.4)
    return lattice_table() * density * (1.0 + spread)


def draw_order_populations(key, part):
    key = jax.random.fold_in(key, 23)
    first_key, second_key = jax.random.split(key)
    phase = jax.random.uniform(first_key, (1, NX, NY, NZ), jnp.float32, -1.0, 1.0)
    spread = jax.random.uniform(second_key, (19, NX, NY, NZ), jnp.float32, -0.5, 0.5)
    return lattice_table() * phase * (1.0 + spread)


def place_ends(drawn, rng, smallest, high):
    longest = drawn.shape.index(max(drawn.shape))
    spots = []
    for shift in (0, 1):
        where = [jax.random.randint(jax.random.fold_in(rng, axis), (), 0, length) for axis, length in enumerate(drawn.shape)]
        where[longest] = (where[longest] + shift) % drawn.shape[longest]
        spots.append(tuple(where))
    return drawn.at[spots[0]].set(smallest).at[spots[1]].set(high)


def setup_inputs(seed: int = 0) -> dict:
    seeds = jax.random.split(jax.random.key(seed), 5)
    fluid_populations = draw_fluid_populations(jax.random.fold_in(seeds[4], 71), 0)
    order_populations = draw_order_populations(jax.random.fold_in(seeds[4], 71), 0)
    plane_offsets = place_ends(jax.random.randint(seeds[2], (STEPS, N_GY), 0, NX), jax.random.fold_in(seeds[2], 1), 0, NX - 1).astype(jnp.int32)
    plane_weights = jnp.clip(jax.random.uniform(seeds[3], (N_GY,), jnp.float32, 0.1, 0.9), 0.1, 0.9)
    return dict(fluid_populations=fluid_populations, order_populations=order_populations, plane_offsets=plane_offsets, plane_weights=plane_weights)


LATTICE_VELOCITIES = [(0, 0, 0), (1, 0, 0), (-1, 0, 0), (0, 1, 0), (0, -1, 0), (0, 0, 1), (0, 0, -1), (1, 1, 0), (-1, -1, 0), (1, -1, 0), (-1, 1, 0), (1, 0, 1), (-1, 0, -1), (1, 0, -1), (-1, 0, 1), (0, 1, 1), (0, -1, -1), (0, 1, -1), (0, -1, 1)]
LATTICE_WEIGHTS = [1.0 / 3.0] + [1.0 / 18.0] * 6 + [1.0 / 36.0] * 12
RISING_SET = [3, 7, 10, 15, 17]
FALLING_SET = [4, 8, 9, 16, 18]
BULK_QUADRATIC = -0.0625
BULK_QUARTIC = 0.0625
STIFFNESS = 0.04
MOBILITY = 0.5
RELAX_FLUID = 0.8
RELAX_ORDER = 0.9
PLANE_SPEED = 0.05


def chemical(extended):
    center = extended[..., 1:-1, 1:-1, 1:-1]
    laplace = (extended[..., 2:, 1:-1, 1:-1] + extended[..., :-2, 1:-1, 1:-1]
               + extended[..., 1:-1, 2:, 1:-1] + extended[..., 1:-1, :-2, 1:-1]
               + extended[..., 1:-1, 1:-1, 2:] + extended[..., 1:-1, 1:-1, :-2] - 6.0 * center)
    potential = BULK_QUADRATIC * center + BULK_QUARTIC * center * center * center - STIFFNESS * laplace
    gradient = jnp.stack([potential[..., 2:, 1:-1, 1:-1] - potential[..., :-2, 1:-1, 1:-1],
                          potential[..., 1:-1, 2:, 1:-1] - potential[..., 1:-1, :-2, 1:-1],
                          potential[..., 1:-1, 1:-1, 2:] - potential[..., 1:-1, 1:-1, :-2]], axis=-4) * 0.5
    return potential[..., 1:-1, 1:-1, 1:-1], gradient


def collide(fluid, order, phase, potential, gradient):
    velocity = jnp.array(LATTICE_VELOCITIES, jnp.float32)
    weights = jnp.array(LATTICE_WEIGHTS, jnp.float32).reshape(19, 1, 1, 1)
    density = jnp.sum(fluid, axis=0)
    momentum = jnp.einsum('iq,ixyz->qxyz', velocity, fluid, precision=lax.Precision.HIGHEST)
    speed = momentum / density
    shifted = speed - RELAX_FLUID * phase * gradient / density
    along = jnp.einsum('iq,qxyz->ixyz', velocity, shifted, precision=lax.Precision.HIGHEST)
    square = jnp.sum(shifted * shifted, axis=0)
    equilibrium = weights * density * (1.0 + 3.0 * along + 4.5 * along * along - 1.5 * square)
    post_fluid = fluid - (fluid - equilibrium) / RELAX_FLUID
    flow = jnp.einsum('iq,qxyz->ixyz', velocity, speed, precision=lax.Precision.HIGHEST)
    order_eq = weights * (3.0 * MOBILITY * potential + 3.0 * phase * flow)
    order_eq = jnp.concatenate([(phase - 2.0 * MOBILITY * potential)[None], order_eq[1:]], axis=0)
    post_order = order - (order - order_eq) / RELAX_ORDER
    return post_fluid, post_order, density


def plane_rows(post_fluid, post_order, density):
    upper_parts = []
    lower_parts = []
    for component in RISING_SET:
        drift = 3.0 * LATTICE_WEIGHTS[component] * LATTICE_VELOCITIES[component][0] * PLANE_SPEED
        upper_parts.append(post_fluid[component, :, -1:, :] - drift * density[:, -1:, :])
    for component in RISING_SET:
        upper_parts.append(post_order[component, :, -1:, :])
    for component in FALLING_SET:
        drift = 3.0 * LATTICE_WEIGHTS[component] * LATTICE_VELOCITIES[component][0] * PLANE_SPEED
        lower_parts.append(post_fluid[component, :, 0:1, :] + drift * density[:, 0:1, :])
    for component in FALLING_SET:
        lower_parts.append(post_order[component, :, 0:1, :])
    return jnp.stack(upper_parts, axis=0), jnp.stack(lower_parts, axis=0)


def assemble(post_fluid, post_order, ghost_low, ghost_high):
    merged = jnp.concatenate([post_fluid, post_order], axis=0)
    rising_all = jnp.array(RISING_SET + [19 + c for c in RISING_SET], jnp.int32)
    falling_all = jnp.array(FALLING_SET + [19 + c for c in FALLING_SET], jnp.int32)
    ghost_shape = (38, merged.shape[1], 1, merged.shape[3])
    lower_ghost = jnp.zeros(ghost_shape, jnp.float32).at[rising_all].set(ghost_low)
    upper_ghost = jnp.zeros(ghost_shape, jnp.float32).at[falling_all].set(ghost_high)
    return jnp.concatenate([lower_ghost, merged, upper_ghost], axis=2)


def propagate(extended):
    count_x = extended.shape[1] - 2
    count_y = extended.shape[2] - 2
    count_z = extended.shape[3] - 2
    moved = []
    for component in range(38):
        step_x, step_y, step_z = LATTICE_VELOCITIES[component % 19]
        moved.append(extended[component, 1 - step_x:1 - step_x + count_x,
                              1 - step_y:1 - step_y + count_y, 1 - step_z:1 - step_z + count_z])
    result = jnp.stack(moved, axis=0)
    return result[:19], result[19:]


def pick_rows(block_rows, indices):
    return jnp.take(block_rows, indices, axis=1)


def slide_rise(rows, shifts, weights):
    across = jnp.arange(NX, dtype=jnp.int32)
    nearer = (across[None, :] - shifts[:, None]) % NX
    farther = (nearer + NX - 1) % NX
    weight = weights[:, None, None, None, None]
    picked = jax.vmap(pick_rows)
    return weight * picked(rows, nearer) + (1.0 - weight) * picked(rows, farther)


def slide_fall(rows, shifts, weights):
    across = jnp.arange(NX, dtype=jnp.int32)
    nearer = (across[None, :] + shifts[:, None]) % NX
    farther = (nearer + 1) % NX
    weight = weights[:, None, None, None, None]
    picked = jax.vmap(pick_rows)
    return weight * picked(rows, nearer) + (1.0 - weight) * picked(rows, farther)


def reference(fluid_populations, order_populations, plane_offsets, plane_weights):
    fluid_blocks = fluid_populations.reshape(19, NX, N_GY, CY, NZ).transpose(2, 0, 1, 3, 4)
    order_blocks = order_populations.reshape(19, NX, N_GY, CY, NZ).transpose(2, 0, 1, 3, 4)
    for step_index in range(STEPS):
        shifts = plane_offsets[step_index].astype(jnp.int32)
        phase = jnp.sum(order_blocks, axis=1)
        upper_rows = phase[:, None, :, CY - 2:, :]
        bottom_rows = phase[:, None, :, :2, :]
        ghost_low = jnp.roll(slide_rise(upper_rows, shifts, plane_weights), 1, axis=0)
        ghost_high = slide_fall(jnp.roll(bottom_rows, -1, axis=0), shifts, plane_weights)
        extended = jnp.concatenate([ghost_low, phase[:, None], ghost_high], axis=3)
        extended = jnp.pad(extended, ((0, 0), (0, 0), (2, 2), (0, 0), (2, 2)), mode="wrap")
        potential, gradient = chemical(extended[:, 0])

        def local_work(items):
            fluid, order, block_phase, block_potential, block_gradient = items
            post_fluid, post_order, density = collide(fluid, order, block_phase, block_potential, block_gradient)
            upper, lower = plane_rows(post_fluid, post_order, density)
            return post_fluid, post_order, upper, lower

        post_fluid, post_order, uppers, lowers = lax.map(local_work, (fluid_blocks, order_blocks, phase, potential, gradient))
        ghost_low = jnp.roll(slide_rise(uppers, shifts, plane_weights), 1, axis=0)
        ghost_high = slide_fall(jnp.roll(lowers, -1, axis=0), shifts, plane_weights)

        def moving(items):
            fluid, order, below_rows, above_rows = items
            grown = assemble(fluid, order, below_rows, above_rows)
            grown = jnp.pad(grown, ((0, 0), (1, 1), (0, 0), (1, 1)), mode="wrap")
            return propagate(grown)

        fluid_blocks, order_blocks = lax.map(moving, (post_fluid, post_order, ghost_low, ghost_high))
    fluid_next = fluid_blocks.transpose(1, 2, 0, 3, 4).reshape(19, NX, NY, NZ)
    order_next = order_blocks.transpose(1, 2, 0, 3, 4).reshape(19, NX, NY, NZ)
    return fluid_next, order_next
```

```python
import jax
import jax.numpy as jnp
from jax import lax
from jax.sharding import PartitionSpec as P

STEPS = 2


LATTICE_VELOCITIES = [
    (0, 0, 0),
    (1, 0, 0),
    (-1, 0, 0),
    (0, 1, 0),
    (0, -1, 0),
    (0, 0, 1),
    (0, 0, -1),
    (1, 1, 0),
    (-1, -1, 0),
    (1, -1, 0),
    (-1, 1, 0),
    (1, 0, 1),
    (-1, 0, -1),
    (1, 0, -1),
    (-1, 0, 1),
    (0, 1, 1),
    (0, -1, -1),
    (0, 1, -1),
    (0, -1, 1),
]
LATTICE_WEIGHTS = [1.0 / 3.0] + [1.0 / 18.0] * 6 + [1.0 / 36.0] * 12
RISING_SET = [3, 7, 10, 15, 17]
FALLING_SET = [4, 8, 9, 16, 18]
BULK_QUADRATIC = -0.0625
BULK_QUARTIC = 0.0625
STIFFNESS = 0.04
MOBILITY = 0.5
RELAX_FLUID = 0.8
RELAX_ORDER = 0.9
PLANE_SPEED = 0.05


def with_halo(cells, sides, width):
    for axis, dim in sides:
        count = lax.axis_size(axis)
        head = lax.slice_in_dim(cells, 0, width, axis=dim)
        tail = lax.slice_in_dim(cells, cells.shape[dim] - width, cells.shape[dim], axis=dim)
        cells = jnp.concatenate(
            [
                lax.ppermute(tail, axis, [(i, (i + 1) % count) for i in range(count)]),
                cells,
                lax.ppermute(head, axis, [((i + 1) % count, i) for i in range(count)]),
            ],
            axis=dim,
        )
    return cells


def chemical(extended):
    center = extended[..., 1:-1, 1:-1, 1:-1]
    laplace = (
        extended[..., 2:, 1:-1, 1:-1]
        + extended[..., :-2, 1:-1, 1:-1]
        + extended[..., 1:-1, 2:, 1:-1]
        + extended[..., 1:-1, :-2, 1:-1]
        + extended[..., 1:-1, 1:-1, 2:]
        + extended[..., 1:-1, 1:-1, :-2]
        - 6.0 * center
    )
    potential = (
        BULK_QUADRATIC * center + BULK_QUARTIC * center * center * center - STIFFNESS * laplace
    )
    gradient = (
        jnp.stack(
            [
                potential[..., 2:, 1:-1, 1:-1] - potential[..., :-2, 1:-1, 1:-1],
                potential[..., 1:-1, 2:, 1:-1] - potential[..., 1:-1, :-2, 1:-1],
                potential[..., 1:-1, 1:-1, 2:] - potential[..., 1:-1, 1:-1, :-2],
            ],
            axis=-4,
        )
        * 0.5
    )
    return (potential[..., 1:-1, 1:-1, 1:-1], gradient)


def collide(fluid, order, phase, potential, gradient):
    velocity = jnp.array(LATTICE_VELOCITIES, jnp.float32)
    weights = jnp.array(LATTICE_WEIGHTS, jnp.float32).reshape(19, 1, 1, 1)
    density = jnp.sum(fluid, axis=0)
    momentum = jnp.einsum("iq,ixyz->qxyz", velocity, fluid, precision=lax.Precision.HIGHEST)
    speed = momentum / density
    shifted = speed - RELAX_FLUID * phase * gradient / density
    along = jnp.einsum("iq,qxyz->ixyz", velocity, shifted, precision=lax.Precision.HIGHEST)
    square = jnp.sum(shifted * shifted, axis=0)
    equilibrium = weights * density * (1.0 + 3.0 * along + 4.5 * along * along - 1.5 * square)
    post_fluid = fluid - (fluid - equilibrium) / RELAX_FLUID
    flow = jnp.einsum("iq,qxyz->ixyz", velocity, speed, precision=lax.Precision.HIGHEST)
    order_eq = weights * (3.0 * MOBILITY * potential + 3.0 * phase * flow)
    order_eq = jnp.concatenate([(phase - 2.0 * MOBILITY * potential)[None], order_eq[1:]], axis=0)
    post_order = order - (order - order_eq) / RELAX_ORDER
    return (post_fluid, post_order, density)


def plane_rows(post_fluid, post_order, density):
    upper_parts = []
    lower_parts = []
    for component in RISING_SET:
        drift = 3.0 * LATTICE_WEIGHTS[component] * LATTICE_VELOCITIES[component][0] * PLANE_SPEED
        upper_parts.append(post_fluid[component, :, -1:, :] - drift * density[:, -1:, :])
    for component in RISING_SET:
        upper_parts.append(post_order[component, :, -1:, :])
    for component in FALLING_SET:
        drift = 3.0 * LATTICE_WEIGHTS[component] * LATTICE_VELOCITIES[component][0] * PLANE_SPEED
        lower_parts.append(post_fluid[component, :, 0:1, :] + drift * density[:, 0:1, :])
    for component in FALLING_SET:
        lower_parts.append(post_order[component, :, 0:1, :])
    return (jnp.stack(upper_parts, axis=0), jnp.stack(lower_parts, axis=0))


def assemble(post_fluid, post_order, ghost_low, ghost_high):
    merged = jnp.concatenate([post_fluid, post_order], axis=0)
    rising_all = jnp.array(RISING_SET + [19 + c for c in RISING_SET], jnp.int32)
    falling_all = jnp.array(FALLING_SET + [19 + c for c in FALLING_SET], jnp.int32)
    ghost_shape = (38, merged.shape[1], 1, merged.shape[3])
    lower_ghost = jnp.zeros(ghost_shape, jnp.float32).at[rising_all].set(ghost_low)
    upper_ghost = jnp.zeros(ghost_shape, jnp.float32).at[falling_all].set(ghost_high)
    return jnp.concatenate([lower_ghost, merged, upper_ghost], axis=2)


def propagate(extended):
    count_x = extended.shape[1] - 2
    count_y = extended.shape[2] - 2
    count_z = extended.shape[3] - 2
    moved = []
    for component in range(38):
        step_x, step_y, step_z = LATTICE_VELOCITIES[component % 19]
        moved.append(
            extended[
                component,
                1 - step_x : 1 - step_x + count_x,
                1 - step_y : 1 - step_y + count_y,
                1 - step_z : 1 - step_z + count_z,
            ]
        )
    result = jnp.stack(moved, axis=0)
    return (result[:19], result[19:])


def plane_pairs(count_x, blocks_y, shift, parity):
    pairs = []
    for place in range(count_x):
        for below in range(parity, blocks_y, 2):
            above = (below + 1) % blocks_y
            pairs.append((place * blocks_y + below, (place + shift) % count_x * blocks_y + above))
            pairs.append((place * blocks_y + above, (place - shift) % count_x * blocks_y + below))
    return pairs


def swap_rows(rows, steps, parity):
    devices_x = lax.axis_size("gx")
    blocks_y = lax.axis_size("gy")

    def branch(shift):
        def run(sent):
            return tuple(
                lax.ppermute(sent, ("gx", "gy"), plane_pairs(devices_x, blocks_y, shift + more, parity))
                for more in (0, 1)
            )

        return run

    return lax.switch(steps, [branch(shift) for shift in range(devices_x)], rows)


def cross(upper, lower, plane_offsets, plane_weights, step_index):
    count_x = upper.shape[1]
    blocks_y = lax.axis_size("gy")
    block = lax.axis_index("gy")
    is_even = block % 2 == 0
    plane_up = block
    plane_down = (block + blocks_y - 1) % blocks_y
    got = []
    for parity in (0, 1):
        above = is_even if parity == 0 else jnp.logical_not(is_even)
        plane = jnp.where(above, plane_up, plane_down)
        steps = plane_offsets[step_index, plane] // count_x
        got.append(swap_rows(jnp.where(above, upper, lower), steps, parity))
    near_fall, far_fall = (jnp.where(is_even, a, b) for a, b in zip(got[0], got[1]))
    near_rise, far_rise = (jnp.where(is_even, b, a) for a, b in zip(got[0], got[1]))
    rest_up = plane_offsets[step_index, plane_down] % count_x
    rest_down = plane_offsets[step_index, plane_up] % count_x
    weight_up = plane_weights[plane_down]
    weight_down = plane_weights[plane_up]
    rise = jnp.concatenate([far_rise, near_rise], axis=1)
    fall = jnp.concatenate([near_fall, far_fall], axis=1)
    ghost_low = weight_up * lax.dynamic_slice_in_dim(rise, count_x - rest_up, count_x, 1) + (
        1.0 - weight_up
    ) * lax.dynamic_slice_in_dim(rise, count_x - 1 - rest_up, count_x, 1)
    ghost_high = weight_down * lax.dynamic_slice_in_dim(fall, rest_down, count_x, 1) + (
        1.0 - weight_down
    ) * lax.dynamic_slice_in_dim(fall, rest_down + 1, count_x, 1)
    return (ghost_low, ghost_high)


def population_edges(grown):
    return with_halo(grown, (("gx", 1), ("gz", 3)), 1)


def per_device(fluid_populations, order_populations, plane_offsets, plane_weights):
    fluid = fluid_populations
    order = order_populations
    for step_index in range(STEPS):
        phase = jnp.sum(order, axis=0)
        count_y = phase.shape[1]
        ghost_low, ghost_high = cross(
            phase[None, :, count_y - 2 :, :],
            phase[None, :, :2, :],
            plane_offsets,
            plane_weights,
            step_index,
        )
        extended = jnp.concatenate([ghost_low, phase[None], ghost_high], axis=2)
        extended = with_halo(extended, (("gx", 1), ("gz", 3)), 2)[0]
        potential, gradient = chemical(extended)
        post_fluid, post_order, density = collide(fluid, order, phase, potential, gradient)
        upper, lower = plane_rows(post_fluid, post_order, density)
        ghost_low, ghost_high = cross(upper, lower, plane_offsets, plane_weights, step_index)
        grown = assemble(post_fluid, post_order, ghost_low, ghost_high)
        grown = population_edges(grown)
        fluid, order = propagate(grown)
    return (fluid, order)


def solution(mesh):
    in_specs = (P(None, "gx", "gy", "gz"), P(None, "gx", "gy", "gz"), P(), P())
    out_specs = (P(None, "gx", "gy", "gz"), P(None, "gx", "gy", "gz"))
    return jax.shard_map(
        per_device, mesh=mesh, in_specs=in_specs, out_specs=out_specs, check_vma=False
    )
```

```python
import functools

import jax
import jax.numpy as jnp
from jax import lax
from jax.experimental import pallas as pl
from jax.experimental.pallas import tpu as pltpu
from jax.sharding import PartitionSpec as P

STEPS = 2

VELOCITIES = [
    (0, 0, 0),
    (1, 0, 0),
    (-1, 0, 0),
    (0, 1, 0),
    (0, -1, 0),
    (0, 0, 1),
    (0, 0, -1),
    (1, 1, 0),
    (-1, -1, 0),
    (1, -1, 0),
    (-1, 1, 0),
    (1, 0, 1),
    (-1, 0, -1),
    (1, 0, -1),
    (-1, 0, 1),
    (0, 1, 1),
    (0, -1, -1),
    (0, 1, -1),
    (0, -1, 1),
]
WEIGHTS = [1.0 / 3.0] + [1.0 / 18.0] * 6 + [1.0 / 36.0] * 12
RISING = [3, 7, 10, 15, 17]
FALLING = [4, 8, 9, 16, 18]
EAST = [i for i, c in enumerate(VELOCITIES) if c[0] == 1]
WEST = [i for i, c in enumerate(VELOCITIES) if c[0] == -1]
FRONT = [i for i, c in enumerate(VELOCITIES) if c[2] == 1]
BACK = [i for i, c in enumerate(VELOCITIES) if c[2] == -1]
A = -0.0625
B = 0.0625
K = 0.04
M = 0.5
TAU_F = 0.8
TAU_G = 0.9
U = 0.05

OWN = 8
BELOW_EDGE = 2
ABOVE_EDGE = 28
ITEMS = 17

VMEM = pl.BlockSpec(memory_space=pltpu.VMEM)
SMEM = pl.BlockSpec(memory_space=pltpu.SMEM)
F32 = jnp.float32


def call(body, outs, operands, specs, scratch=(), name=None):
    return pl.pallas_call(
        body,
        out_shape=[jax.ShapeDtypeStruct(shape, F32) for shape in outs],
        in_specs=specs,
        out_specs=[VMEM] * len(outs),
        scratch_shapes=list(scratch),
        compiler_params=pltpu.CompilerParams(vmem_limit_bytes=32 * 1024 * 1024),
        name=name,
    )(*operands)


def lanes(shape):
    return lax.broadcasted_iota(jnp.int32, shape, 1)


def rows_of(shape):
    return lax.broadcasted_iota(jnp.int32, shape, 0)


def shift(value, amount, axis):
    amount = amount % value.shape[axis]
    return value if amount == 0 else pltpu.roll(value, amount, axis)


def plane_shift(offsets, step, plane):
    return lax.rem(offsets[step, plane] + 2, 4) - 2


def neighbours():
    block = lax.axis_index("gy")
    return block, lax.rem(block + 3, 4), lax.rem(block, 2)


def edge_messages(fluid, order, phase_ref, even_ref, odd_ref):
    odd_block = neighbours()[2] == 1

    def put(item, x, low, high):
        even_ref[item, x : x + 1, :] = jnp.where(odd_block, low, high)
        odd_ref[item, x : x + 1, :] = jnp.where(odd_block, high, low)

    for x in range(4):
        f = [fluid(i, x) for i in range(19)]
        g = [order(i, x) for i in range(19)]
        phase = sum(g[1:], g[0])
        phase_ref[x] = phase
        for item in range(3):
            put(item, x, phase[item : item + 1], phase[13 + item : 14 + item])
        fields = [sum(f[1:], f[0])]
        for q in range(3):
            plus = [f[i] for i, c in enumerate(VELOCITIES) if c[q] == 1]
            minus = [f[i] for i, c in enumerate(VELOCITIES) if c[q] == -1]
            fields.append(sum(plus[1:], plus[0]) - sum(minus[1:], minus[0]))
        for n, field in enumerate(fields):
            put(3 + n, x, field[0:1], field[15:16])
        for n in range(5):
            put(7 + n, x, f[FALLING[n]][0:1], f[RISING[n]][15:16])
            put(12 + n, x, g[FALLING[n]][0:1], g[RISING[n]][15:16])


def first_kernel(f_ref, g_ref, phase_ref, even_ref, odd_ref):
    edge_messages(
        lambda i, x: f_ref[i, x], lambda i, x: g_ref[i, x], phase_ref, even_ref, odd_ref
    )


def stack_kernel(phase_ref, even_ref, odd_ref, stack_ref, edge_ref):
    odd_block = neighbours()[2] == 1
    stack_ref[...] = jnp.zeros_like(stack_ref)
    for x in range(4):
        stack_ref[x, OWN : OWN + 16, :] = phase_ref[x]
    for item in range(ITEMS):
        below = jnp.where(odd_block, even_ref[item], odd_ref[item])
        above = jnp.where(odd_block, odd_ref[item], even_ref[item])
        if item < 3:
            for x in range(4):
                stack_ref[x, item : item + 1, :] = below[x : x + 1]
                stack_ref[x, ABOVE_EDGE + item : ABOVE_EDGE + item + 1, :] = above[x : x + 1]
        else:
            edge_ref[item - 3, 0:4, :] = below
            edge_ref[item - 3, 4:8, :] = above


def ghost_kernel(
    step, offsets, weights, own_ref, west_ref, east_ref, phase_ref, first_ref, last_ref, wide
):
    block, down, _ = neighbours()
    r_down = plane_shift(offsets, step, down)
    r_up = plane_shift(offsets, step, block)
    w_down = weights[down]
    w_up = weights[block]
    wide[0:4] = west_ref[...]
    wide[4:8] = own_ref[...]
    wide[8:12] = east_ref[...]
    shape = (32, 128)
    row = rows_of(shape)
    lane = lanes(shape)
    first = jnp.zeros(shape, F32)
    last = jnp.zeros(shape, F32)

    def rise(place, r, w):
        return w * wide[place - r] + (1.0 - w) * wide[place - r - 1]

    def fall(place, r, w):
        return w * wide[place + r] + (1.0 - w) * wide[place + r + 1]

    for n in range(8):
        place = n + 2
        value = wide[place]
        if 1 <= n <= 6:
            value = jnp.where((row == 6) | (row == 7), shift(rise(place, r_down, w_down), 5, 0), value)
            value = jnp.where((row == 3) | (row == 4), shift(fall(place, r_down, w_down), -5, 0), value)
            value = jnp.where((row == 24) | (row == 25), shift(fall(place, r_up, w_up), -4, 0), value)
            value = jnp.where((row == 26) | (row == 27), shift(rise(place, r_up, w_up), 4, 0), value)
        phase_ref[n] = value
        first = jnp.where(lane // 2 == n, shift(value, 2 * n, 1), first)
        last = jnp.where(lane // 2 == n, shift(value, 2 * n - 126, 1), last)
    first_ref[...] = first
    last_ref[...] = last


def bulk_potential(phase, around):
    return A * phase + B * phase * phase * phase - K * (around - 6.0 * phase)


def collide_kernel(
    phase_ref,
    first_ref,
    last_ref,
    left_ref,
    right_ref,
    edge_ref,
    f_ref,
    g_ref,
    post_ref,
    east_ref,
    west_ref,
    ghost,
    pots,
):
    shape = (32, 128)
    lane = lanes(shape)
    left = left_ref[...]
    right = right_ref[...]
    first = first_ref[...]
    last = last_ref[...]

    def updown(value):
        return shift(value, 1, 0) + shift(value, -1, 0)

    left_pot = bulk_potential(
        left, shift(left, 2, 1) + shift(left, -2, 1) + updown(left) + shift(left, 1, 1) + shift(first, 1, 1)
    )
    right_pot = bulk_potential(
        right,
        shift(right, 2, 1) + shift(right, -2, 1) + updown(right) + shift(right, -1, 1) + shift(last, -1, 1),
    )
    for n in range(1, 7):
        value = phase_ref[n]
        before = jnp.where(lane == 0, shift(left, -(2 * n + 1), 1), shift(value, 1, 1))
        after = jnp.where(lane == 127, shift(right, 127 - 2 * n, 1), shift(value, -1, 1))
        around = phase_ref[n - 1] + phase_ref[n + 1] + updown(value) + before + after
        pots[n] = bulk_potential(value, around)

    for x in range(4):
        n = x + 2
        phase_all = phase_ref[n]
        pot_all = pots[n]
        gx_all = 0.5 * (pots[n + 1] - pots[n - 1])
        gy_all = 0.5 * (shift(pot_all, -1, 0) - shift(pot_all, 1, 0))
        before = jnp.where(lane == 0, shift(left_pot, -(2 * n + 1), 1), shift(pot_all, 1, 1))
        after = jnp.where(lane == 127, shift(right_pot, 127 - 2 * n, 1), shift(pot_all, -1, 1))
        gz_all = 0.5 * (after - before)
        for k, value in enumerate((phase_all, pot_all, gx_all, gy_all, gz_all)):
            ghost[k, x : x + 1, :] = value[BELOW_EDGE : BELOW_EDGE + 1]
            ghost[k, 4 + x : 5 + x, :] = value[ABOVE_EDGE : ABOVE_EDGE + 1]
        own = slice(OWN, OWN + 16)
        phase = phase_all[own]
        pot = pot_all[own]
        grad = (gx_all[own], gy_all[own], gz_all[own])

        f = [f_ref[i, x] for i in range(19)]
        density = sum(f[1:], f[0])
        momentum = []
        for q in range(3):
            plus = [f[i] for i, c in enumerate(VELOCITIES) if c[q] == 1]
            minus = [f[i] for i, c in enumerate(VELOCITIES) if c[q] == -1]
            momentum.append(sum(plus[1:], plus[0]) - sum(minus[1:], minus[0]))
        inverse = 1.0 / density
        speed = [m * inverse for m in momentum]
        force = TAU_F * phase * inverse
        shifted = [s - force * d for s, d in zip(speed, grad)]
        square = shifted[0] * shifted[0] + shifted[1] * shifted[1] + shifted[2] * shifted[2]
        rest = 1.0 - 1.5 * square
        keep_f = 1.0 - 1.0 / TAU_F
        keep_g = 1.0 - 1.0 / TAU_G

        def store(i, fs, gs):
            post_ref[i, x] = fs
            post_ref[19 + i, x] = gs
            if x == 3 and i in EAST:
                k = EAST.index(i)
                east_ref[k, 0:16, :] = fs
                east_ref[5 + k, 0:16, :] = gs
            if x == 0 and i in WEST:
                k = WEST.index(i)
                west_ref[k, 0:16, :] = fs
                west_ref[5 + k, 0:16, :] = gs

        store(
            0,
            keep_f * f[0] + (WEIGHTS[0] / TAU_F) * density * rest,
            keep_g * g_ref[0, x] + (1.0 / TAU_G) * (phase - 2.0 * M * pot),
        )
        flow_scale = 3.0 * phase
        for i in range(1, 19, 2):
            along = directed(VELOCITIES[i], shifted)
            flow = directed(VELOCITIES[i], speed)
            scale = (WEIGHTS[i] / TAU_F) * density
            even = scale * (rest + 4.5 * along * along)
            odd = scale * (3.0 * along)
            g_even = (WEIGHTS[i] / TAU_G * 3.0 * M) * pot
            g_odd = (WEIGHTS[i] / TAU_G) * (flow_scale * flow)
            store(i, keep_f * f[i] + (even + odd), keep_g * g_ref[i, x] + (g_even + g_odd))
            store(i + 1, keep_f * f[i + 1] + (even - odd), keep_g * g_ref[i + 1, x] + (g_even - g_odd))

    sign = jnp.where(rows_of((8, 128)) < 4, 1.0, -1.0)
    phase, pot, gx, gy, gz = (ghost[k] for k in range(5))
    density = edge_ref[0]
    inverse = 1.0 / density
    speed = [edge_ref[1 + q] * inverse for q in range(3)]
    force = TAU_F * phase * inverse
    shifted = [s - force * d for s, d in zip(speed, (gx, gy, gz))]
    square = shifted[0] * shifted[0] + shifted[1] * shifted[1] + shifted[2] * shifted[2]
    rest = 1.0 - 1.5 * square
    for k, i in enumerate(RISING):
        along = sign * directed(VELOCITIES[i], shifted)
        flow = sign * directed(VELOCITIES[i], speed)
        feq = WEIGHTS[i] * density * (rest + 3.0 * along + 4.5 * along * along)
        fs = (1.0 - 1.0 / TAU_F) * edge_ref[4 + k] + (1.0 / TAU_F) * feq
        fs = fs - (3.0 * WEIGHTS[i] * VELOCITIES[i][0] * U) * density
        geq = WEIGHTS[i] * (3.0 * M * pot + 3.0 * phase * flow)
        gs = (1.0 - 1.0 / TAU_G) * edge_ref[9 + k] + (1.0 / TAU_G) * geq
        for ref in (east_ref, west_ref):
            ref[k, 16:24, :] = fs
            ref[5 + k, 16:24, :] = gs


def directed(velocity, parts):
    total = None
    for c, part in zip(velocity, parts):
        if c == 1:
            total = part if total is None else total + part
        elif c == -1:
            total = -part if total is None else total - part
    return total


def stream_kernel(
    step, offsets, weights, post_ref, own_ref, from_west, from_east, out_ref, first_ref, last_ref, wide
):
    block, down, _ = neighbours()
    r_down = plane_shift(offsets, step, down)
    r_up = plane_shift(offsets, step, block)
    w_down = weights[down]
    w_up = weights[block]
    for k in range(10):
        for side, (low, high) in enumerate(((16, 20), (20, 24))):
            for place, ref in enumerate((from_west, own_ref, from_east)):
                for x in range(4):
                    wide[side, 4 * place + x, k : k + 1, :] = ref[k, low + x : low + x + 1, :]
    shape = (16, 128)
    row = rows_of(shape)
    lane = lanes(shape)
    first = jnp.zeros(shape, F32)
    last = jnp.zeros(shape, F32)
    for x in range(4):
        place = x + 4
        risen = {}
        fallen = {}
        for c in (-1, 0, 1):
            at = place - c - r_down
            risen[c] = w_down * wide[0, at] + (1.0 - w_down) * wide[0, at - 1]
            at = place - c + r_up
            fallen[c] = w_up * wide[1, at] + (1.0 - w_up) * wide[1, at + 1]
        for i in range(38):
            part, component = divmod(i, 19)
            cx, cy, cz = VELOCITIES[component]
            source = x - cx
            if source < 0:
                value = from_west[5 * part + EAST.index(component), 0:16, :]
            elif source > 3:
                value = from_east[5 * part + WEST.index(component), 0:16, :]
            else:
                value = post_ref[i, source]
            if cy == 1:
                k = 5 * part + RISING.index(component)
                value = jnp.where(row == 0, risen[cx][k : k + 1], shift(value, 1, 0))
            elif cy == -1:
                k = 5 * part + FALLING.index(component)
                value = jnp.where(row == 15, fallen[cx][k : k + 1], shift(value, -1, 0))
            out_ref[i, x] = value
            if cz == 1:
                at = 4 * (5 * part + FRONT.index(component)) + x
                last = jnp.where(lane == at, shift(value, at - 127, 1), last)
            elif cz == -1:
                at = 4 * (5 * part + BACK.index(component)) + x
                first = jnp.where(lane == at, shift(value, at, 1), first)
    first_ref[...] = first
    last_ref[...] = last


def finish_kernel(more, moved_ref, left_ref, right_ref, f_ref, g_ref, *rest):
    lane = lanes((16, 128))
    left = left_ref[...]
    right = right_ref[...]
    for x in range(4):
        for i in range(38):
            part, component = divmod(i, 19)
            value = moved_ref[i, x]
            cz = VELOCITIES[component][2]
            if cz == 1:
                at = 4 * (5 * part + FRONT.index(component)) + x
                value = jnp.where(lane == 0, shift(left, -at, 1), shift(value, 1, 1))
            elif cz == -1:
                at = 4 * (5 * part + BACK.index(component)) + x
                value = jnp.where(lane == 127, shift(right, 127 - at, 1), shift(value, -1, 1))
            (g_ref if part else f_ref)[component, x] = value
    if more:
        edge_messages(lambda i, x: f_ref[i, x], lambda i, x: g_ref[i, x], *rest)


def both_ways(axis, forward, backward):
    count = lax.axis_size(axis)
    return (
        lax.ppermute(forward, axis, [(i, (i + 1) % count) for i in range(count)]),
        lax.ppermute(backward, axis, [((i + 1) % count, i) for i in range(count)]),
    )


def plane_pairs(count_x, blocks_y, steps, parity):
    pairs = []
    for place in range(count_x):
        for below in range(parity, blocks_y, 2):
            above = (below + 1) % blocks_y
            pairs.append((place * blocks_y + below, (place + steps) % count_x * blocks_y + above))
            pairs.append((place * blocks_y + above, (place - steps) % count_x * blocks_y + below))
    return pairs


def swap_rows(rows, steps, parity):
    devices_x = lax.axis_size("gx")
    blocks_y = lax.axis_size("gy")

    def branch(number):
        pairs = plane_pairs(devices_x, blocks_y, number, parity)
        return lambda sent: lax.ppermute(sent, ("gx", "gy"), pairs)

    return lax.switch(steps, [branch(number) for number in range(devices_x)], rows)


def per_device(fluid, order, offsets, weights):
    block = lax.axis_index("gy")
    planes = (block // 2 * 2, (block + 3) % 4 // 2 * 2 + 1)
    state = (19, 4, 16, 128)
    rows = (ITEMS, 4, 128)
    phase, even, odd = call(
        first_kernel, [(4, 16, 128), rows, rows], (fluid, order), [VMEM] * 2, name="moments"
    )
    for step in range(STEPS):
        even = swap_rows(even, (offsets[step, planes[0]] + 2) // 4 % 16, 0)
        odd = swap_rows(odd, (offsets[step, planes[1]] + 2) // 4 % 16, 1)
        stack, edge = call(
            stack_kernel,
            [(4, 32, 128), (ITEMS - 3, 8, 128)],
            (phase, even, odd),
            [VMEM] * 3,
            name="stack",
        )
        west, east = both_ways("gx", stack, stack)
        wide, first, last = call(
            functools.partial(ghost_kernel, step),
            [(8, 32, 128), (32, 128), (32, 128)],
            (offsets, weights, stack, west, east),
            [SMEM] * 2 + [VMEM] * 3,
            [pltpu.VMEM((12, 32, 128), F32)],
            name="ghosts",
        )
        left, right = both_ways("gz", last, first)
        post, to_east, to_west = call(
            collide_kernel,
            [(38, 4, 16, 128), (10, 24, 128), (10, 24, 128)],
            (wide, first, last, left, right, edge, fluid, order),
            [VMEM] * 8,
            [pltpu.VMEM((5, 8, 128), F32), pltpu.VMEM((8, 32, 128), F32)],
            name="collide",
        )
        west, east = both_ways("gx", to_east, to_west)
        moved, first, last = call(
            functools.partial(stream_kernel, step),
            [(38, 4, 16, 128), (16, 128), (16, 128)],
            (offsets, weights, post, to_east, west, east),
            [SMEM] * 2 + [VMEM] * 4,
            [pltpu.VMEM((2, 12, 16, 128), F32)],
            name="stream",
        )
        left, right = both_ways("gz", last, first)
        more = step + 1 < STEPS
        outs = call(
            functools.partial(finish_kernel, more),
            [state, state] + ([(4, 16, 128), rows, rows] if more else []),
            (moved, left, right),
            [VMEM] * 3,
            name="finish",
        )
        fluid, order = outs[:2]
        if more:
            phase, even, odd = outs[2:]
    return (fluid, order)


def solution(mesh):
    in_specs = (P(None, "gx", "gy", "gz"), P(None, "gx", "gy", "gz"), P(), P())
    out_specs = (P(None, "gx", "gy", "gz"), P(None, "gx", "gy", "gz"))
    return jax.shard_map(
        per_device, mesh=mesh, in_specs=in_specs, out_specs=out_specs, check_vma=False
    )
```

```python
import functools

import jax
import jax.numpy as jnp
from jax import lax
from jax.experimental import pallas as pl
from jax.experimental.pallas import tpu as pltpu
from jax.sharding import PartitionSpec as P

STEPS = 2

VELOCITIES = [
    (0, 0, 0),
    (1, 0, 0),
    (-1, 0, 0),
    (0, 1, 0),
    (0, -1, 0),
    (0, 0, 1),
    (0, 0, -1),
    (1, 1, 0),
    (-1, -1, 0),
    (1, -1, 0),
    (-1, 1, 0),
    (1, 0, 1),
    (-1, 0, -1),
    (1, 0, -1),
    (-1, 0, 1),
    (0, 1, 1),
    (0, -1, -1),
    (0, 1, -1),
    (0, -1, 1),
]
WEIGHTS = [1.0 / 3.0] + [1.0 / 18.0] * 6 + [1.0 / 36.0] * 12
RISING = [3, 7, 10, 15, 17]
FALLING = [4, 8, 9, 16, 18]
EAST = [i for i, c in enumerate(VELOCITIES) if c[0] == 1]
WEST = [i for i, c in enumerate(VELOCITIES) if c[0] == -1]
FRONT = [i for i, c in enumerate(VELOCITIES) if c[2] == 1]
BACK = [i for i, c in enumerate(VELOCITIES) if c[2] == -1]
A = -0.0625
B = 0.0625
K = 0.04
M = 0.5
TAU_F = 0.8
TAU_G = 0.9
U = 0.05

OWN = 8
BELOW_EDGE = 2
ABOVE_EDGE = 28
ITEMS = 17

VMEM = pl.BlockSpec(memory_space=pltpu.VMEM)
SMEM = pl.BlockSpec(memory_space=pltpu.SMEM)
F32 = jnp.float32


def call(body, outs, operands, specs, scratch=(), name=None):
    return pl.pallas_call(
        body,
        out_shape=[jax.ShapeDtypeStruct(shape, F32) for shape in outs],
        in_specs=specs,
        out_specs=[VMEM] * len(outs),
        scratch_shapes=list(scratch),
        compiler_params=pltpu.CompilerParams(vmem_limit_bytes=32 * 1024 * 1024),
        name=name,
    )(*operands)


def lanes(shape):
    return lax.broadcasted_iota(jnp.int32, shape, 1)


def rows_of(shape):
    return lax.broadcasted_iota(jnp.int32, shape, 0)


def shift(value, amount, axis):
    amount = amount % value.shape[axis]
    return value if amount == 0 else pltpu.roll(value, amount, axis)


def plane_shift(offsets, step, plane):
    return lax.rem(offsets[step, plane] + 2, 4) - 2


def planes():
    block = lax.axis_index("gy")
    return block, lax.rem(block + 3, 4)


def is_odd(axis):
    return lax.rem(lax.axis_index(axis), 2) == 1


def swapped(odd, one, two):
    return jnp.where(odd, two, one), jnp.where(odd, one, two)


def edge_messages(fluid, order, phase_ref, keep_ref, give_ref):
    odd = is_odd("gz")

    def put(item, x, low, high):
        keep, give = swapped(odd, high, low)
        keep_ref[item, x : x + 1, :] = keep
        give_ref[item, x : x + 1, :] = give

    for x in range(4):
        f = [fluid(i, x) for i in range(19)]
        g = [order(i, x) for i in range(19)]
        phase = sum(g[1:], g[0])
        phase_ref[x] = phase
        for item in range(3):
            put(item, x, phase[item : item + 1], phase[13 + item : 14 + item])
        fields = [sum(f[1:], f[0])]
        for q in range(3):
            plus = [f[i] for i, c in enumerate(VELOCITIES) if c[q] == 1]
            minus = [f[i] for i, c in enumerate(VELOCITIES) if c[q] == -1]
            fields.append(sum(plus[1:], plus[0]) - sum(minus[1:], minus[0]))
        for n, field in enumerate(fields):
            put(3 + n, x, field[0:1], field[15:16])
        for n in range(5):
            put(7 + n, x, f[FALLING[n]][0:1], f[RISING[n]][15:16])
            put(12 + n, x, g[FALLING[n]][0:1], g[RISING[n]][15:16])


def first_kernel(f_ref, g_ref, *rest):
    edge_messages(lambda i, x: f_ref[i, x], lambda i, x: g_ref[i, x], *rest)


def pair_kernel(keep_ref, got_ref, pair_ref):
    pair_ref[0] = keep_ref[...]
    pair_ref[1] = got_ref[...]


def stack_kernel(phase_ref, crossed_ref, other_ref, stack_ref, edge_ref):
    odd = is_odd("gz")
    stack_ref[...] = jnp.zeros_like(stack_ref)
    for x in range(4):
        stack_ref[x, OWN : OWN + 16, :] = phase_ref[x]
    for item in range(ITEMS):
        above, below = swapped(odd, crossed_ref[1, item], other_ref[0, item])
        if item < 3:
            for x in range(4):
                stack_ref[x, item : item + 1, :] = below[x : x + 1]
                stack_ref[x, ABOVE_EDGE + item : ABOVE_EDGE + item + 1, :] = above[x : x + 1]
        else:
            edge_ref[item - 3, 0:4, :] = below
            edge_ref[item - 3, 4:8, :] = above


def ghost_kernel(
    step, offsets, weights, own_ref, one_ref, two_ref, phase_ref, send_one, send_two, wide
):
    up, down = planes()
    r_down = plane_shift(offsets, step, down)
    r_up = plane_shift(offsets, step, up)
    w_down = weights[down]
    w_up = weights[up]
    odd = is_odd("gx")
    wide[4:8] = own_ref[...]
    for x in range(4):
        east, west = swapped(odd, one_ref[x], two_ref[x])
        wide[x] = west
        wide[8 + x] = east
    shape = (32, 128)
    row = rows_of(shape)
    lane = lanes(shape)
    first = jnp.zeros(shape, F32)
    last = jnp.zeros(shape, F32)

    def rise(place, r, w):
        return w * wide[place - r] + (1.0 - w) * wide[place - r - 1]

    def fall(place, r, w):
        return w * wide[place + r] + (1.0 - w) * wide[place + r + 1]

    for n in range(8):
        place = n + 2
        value = wide[place]
        if 1 <= n <= 6:
            value = jnp.where((row == 6) | (row == 7), shift(rise(place, r_down, w_down), 5, 0), value)
            value = jnp.where((row == 3) | (row == 4), shift(fall(place, r_down, w_down), -5, 0), value)
            value = jnp.where((row == 24) | (row == 25), shift(fall(place, r_up, w_up), -4, 0), value)
            value = jnp.where((row == 26) | (row == 27), shift(rise(place, r_up, w_up), 4, 0), value)
        phase_ref[n] = value
        first = jnp.where(lane // 2 == n, shift(value, 2 * n, 1), first)
        last = jnp.where(lane // 2 == n, shift(value, 2 * n - 126, 1), last)
    send_one[...], send_two[...] = swapped(is_odd("gz"), last, first)


def bulk_potential(phase, around):
    return A * phase + B * phase * phase * phase - K * (around - 6.0 * phase)


def collide_kernel(
    phase_ref,
    sent_one,
    sent_two,
    got_one,
    got_two,
    edge_ref,
    f_ref,
    g_ref,
    post_ref,
    send_one,
    send_two,
    ghost,
    pots,
    east,
    west,
):
    shape = (32, 128)
    lane = lanes(shape)
    odd = is_odd("gz")
    last, first = swapped(odd, sent_one[...], sent_two[...])
    right, left = swapped(odd, got_one[...], got_two[...])

    def updown(value):
        return shift(value, 1, 0) + shift(value, -1, 0)

    left_pot = bulk_potential(
        left, shift(left, 2, 1) + shift(left, -2, 1) + updown(left) + shift(left, 1, 1) + shift(first, 1, 1)
    )
    right_pot = bulk_potential(
        right,
        shift(right, 2, 1) + shift(right, -2, 1) + updown(right) + shift(right, -1, 1) + shift(last, -1, 1),
    )
    for n in range(1, 7):
        value = phase_ref[n]
        before = jnp.where(lane == 0, shift(left, -(2 * n + 1), 1), shift(value, 1, 1))
        after = jnp.where(lane == 127, shift(right, 127 - 2 * n, 1), shift(value, -1, 1))
        around = phase_ref[n - 1] + phase_ref[n + 1] + updown(value) + before + after
        pots[n] = bulk_potential(value, around)

    for x in range(4):
        n = x + 2
        phase_all = phase_ref[n]
        pot_all = pots[n]
        gx_all = 0.5 * (pots[n + 1] - pots[n - 1])
        gy_all = 0.5 * (shift(pot_all, -1, 0) - shift(pot_all, 1, 0))
        before = jnp.where(lane == 0, shift(left_pot, -(2 * n + 1), 1), shift(pot_all, 1, 1))
        after = jnp.where(lane == 127, shift(right_pot, 127 - 2 * n, 1), shift(pot_all, -1, 1))
        gz_all = 0.5 * (after - before)
        for k, value in enumerate((phase_all, pot_all, gx_all, gy_all, gz_all)):
            ghost[k, x : x + 1, :] = value[BELOW_EDGE : BELOW_EDGE + 1]
            ghost[k, 4 + x : 5 + x, :] = value[ABOVE_EDGE : ABOVE_EDGE + 1]
        own = slice(OWN, OWN + 16)
        phase = phase_all[own]
        pot = pot_all[own]
        grad = (gx_all[own], gy_all[own], gz_all[own])

        f = [f_ref[i, x] for i in range(19)]
        density = sum(f[1:], f[0])
        momentum = []
        for q in range(3):
            plus = [f[i] for i, c in enumerate(VELOCITIES) if c[q] == 1]
            minus = [f[i] for i, c in enumerate(VELOCITIES) if c[q] == -1]
            momentum.append(sum(plus[1:], plus[0]) - sum(minus[1:], minus[0]))
        inverse = 1.0 / density
        speed = [m * inverse for m in momentum]
        force = TAU_F * phase * inverse
        shifted = [s - force * d for s, d in zip(speed, grad)]
        square = shifted[0] * shifted[0] + shifted[1] * shifted[1] + shifted[2] * shifted[2]
        rest = 1.0 - 1.5 * square
        keep_f = 1.0 - 1.0 / TAU_F
        keep_g = 1.0 - 1.0 / TAU_G

        def store(i, fs, gs):
            post_ref[i, x] = fs
            post_ref[19 + i, x] = gs
            if x == 3 and i in EAST:
                k = EAST.index(i)
                east[k] = fs
                east[5 + k] = gs
            if x == 0 and i in WEST:
                k = WEST.index(i)
                west[k] = fs
                west[5 + k] = gs

        store(
            0,
            keep_f * f[0] + (WEIGHTS[0] / TAU_F) * density * rest,
            keep_g * g_ref[0, x] + (1.0 / TAU_G) * (phase - 2.0 * M * pot),
        )
        flow_scale = 3.0 * phase
        for i in range(1, 19, 2):
            along = directed(VELOCITIES[i], shifted)
            flow = directed(VELOCITIES[i], speed)
            scale = (WEIGHTS[i] / TAU_F) * density
            even = scale * (rest + 4.5 * along * along)
            odd = scale * (3.0 * along)
            g_even = (WEIGHTS[i] / TAU_G * 3.0 * M) * pot
            g_odd = (WEIGHTS[i] / TAU_G) * (flow_scale * flow)
            store(i, keep_f * f[i] + (even + odd), keep_g * g_ref[i, x] + (g_even + g_odd))
            store(i + 1, keep_f * f[i + 1] + (even - odd), keep_g * g_ref[i + 1, x] + (g_even - g_odd))

    sign = jnp.where(rows_of((8, 128)) < 4, 1.0, -1.0)
    phase, pot, gx, gy, gz = (ghost[k] for k in range(5))
    density = edge_ref[0]
    inverse = 1.0 / density
    speed = [edge_ref[1 + q] * inverse for q in range(3)]
    force = TAU_F * phase * inverse
    shifted = [s - force * d for s, d in zip(speed, (gx, gy, gz))]
    square = shifted[0] * shifted[0] + shifted[1] * shifted[1] + shifted[2] * shifted[2]
    rest = 1.0 - 1.5 * square
    for k, i in enumerate(RISING):
        along = sign * directed(VELOCITIES[i], shifted)
        flow = sign * directed(VELOCITIES[i], speed)
        feq = WEIGHTS[i] * density * (rest + 3.0 * along + 4.5 * along * along)
        fs = (1.0 - 1.0 / TAU_F) * edge_ref[4 + k] + (1.0 / TAU_F) * feq
        fs = fs - (3.0 * WEIGHTS[i] * VELOCITIES[i][0] * U) * density
        geq = WEIGHTS[i] * (3.0 * M * pot + 3.0 * phase * flow)
        gs = (1.0 - 1.0 / TAU_G) * edge_ref[9 + k] + (1.0 / TAU_G) * geq
        for ref in (send_one, send_two):
            ref[k, 16:24, :] = fs
            ref[5 + k, 16:24, :] = gs
    odd = is_odd("gx")
    for k in range(10):
        send_one[k, 0:16, :], send_two[k, 0:16, :] = swapped(odd, east[k], west[k])


def directed(velocity, parts):
    total = None
    for c, part in zip(velocity, parts):
        if c == 1:
            total = part if total is None else total + part
        elif c == -1:
            total = -part if total is None else total - part
    return total


def stream_kernel(
    step, offsets, weights, post_ref, own_ref, one_ref, two_ref, out_ref, send_one, send_two, wide
):
    up, down = planes()
    r_down = plane_shift(offsets, step, down)
    r_up = plane_shift(offsets, step, up)
    w_down = weights[down]
    w_up = weights[up]
    odd = is_odd("gx")
    for k in range(10):
        from_east, from_west = swapped(odd, one_ref[k, 16:24, :], two_ref[k, 16:24, :])
        for place, rows in enumerate((from_west, own_ref[k, 16:24, :], from_east)):
            for side in (0, 1):
                for x in range(4):
                    at = 4 * side + x
                    wide[side, 4 * place + x, k : k + 1, :] = rows[at : at + 1]
    shape = (16, 128)
    row = rows_of(shape)
    lane = lanes(shape)
    first = jnp.zeros(shape, F32)
    last = jnp.zeros(shape, F32)
    for x in range(4):
        place = x + 4
        risen = {}
        fallen = {}
        for c in (-1, 0, 1):
            at = place - c - r_down
            risen[c] = w_down * wide[0, at] + (1.0 - w_down) * wide[0, at - 1]
            at = place - c + r_up
            fallen[c] = w_up * wide[1, at] + (1.0 - w_up) * wide[1, at + 1]
        for i in range(38):
            part, component = divmod(i, 19)
            cx, cy, cz = VELOCITIES[component]
            source = x - cx
            if source < 0:
                k = 5 * part + EAST.index(component)
                value = jnp.where(odd, one_ref[k, 0:16, :], two_ref[k, 0:16, :])
            elif source > 3:
                k = 5 * part + WEST.index(component)
                value = jnp.where(odd, two_ref[k, 0:16, :], one_ref[k, 0:16, :])
            else:
                value = post_ref[i, source]
            if cy == 1:
                k = 5 * part + RISING.index(component)
                value = jnp.where(row == 0, risen[cx][k : k + 1], shift(value, 1, 0))
            elif cy == -1:
                k = 5 * part + FALLING.index(component)
                value = jnp.where(row == 15, fallen[cx][k : k + 1], shift(value, -1, 0))
            out_ref[i, x] = value
            if cz == 1:
                at = 4 * (5 * part + FRONT.index(component)) + x
                last = jnp.where(lane == at, shift(value, at - 127, 1), last)
            elif cz == -1:
                at = 4 * (5 * part + BACK.index(component)) + x
                first = jnp.where(lane == at, shift(value, at, 1), first)
    send_one[...], send_two[...] = swapped(is_odd("gz"), last, first)


def finish_kernel(more, moved_ref, one_ref, two_ref, f_ref, g_ref, *rest):
    lane = lanes((16, 128))
    right, left = swapped(is_odd("gz"), one_ref[...], two_ref[...])
    for x in range(4):
        for i in range(38):
            part, component = divmod(i, 19)
            value = moved_ref[i, x]
            cz = VELOCITIES[component][2]
            if cz == 1:
                at = 4 * (5 * part + FRONT.index(component)) + x
                value = jnp.where(lane == 0, shift(left, -at, 1), shift(value, 1, 1))
            elif cz == -1:
                at = 4 * (5 * part + BACK.index(component)) + x
                value = jnp.where(lane == 127, shift(right, 127 - at, 1), shift(value, -1, 1))
            (g_ref if part else f_ref)[component, x] = value
    if more:
        edge_messages(lambda i, x: f_ref[i, x], lambda i, x: g_ref[i, x], *rest)


def swap(axis, values, parity):
    count = lax.axis_size(axis)
    pairs = []
    for low in range(parity, count, 2):
        high = (low + 1) % count
        pairs += [(low, high), (high, low)]
    return lax.ppermute(values, axis, pairs)


def plane_pairs(count_x, blocks_y, count_z, steps):
    def number(x, y, z):
        return (x % count_x * blocks_y + y % blocks_y) * count_z + z

    pairs = []
    for x in range(count_x):
        for y in range(blocks_y):
            for z in range(0, count_z, 2):
                pairs.append((number(x, y, z), number(x + steps, y + 1, z + 1)))
                pairs.append((number(x + steps, y + 1, z + 1), number(x, y, z)))
    return pairs


def cross_planes(rows, steps):
    axes = ("gx", "gy", "gz")
    sizes = [lax.axis_size(axis) for axis in axes]

    def branch(number):
        pairs = plane_pairs(*sizes, number)
        return lambda sent: lax.ppermute(sent, axes, pairs)

    return lax.switch(steps, [branch(number) for number in range(sizes[0])], rows)


def per_device(fluid, order, offsets, weights):
    plane = (lax.axis_index("gy") + 3 * (lax.axis_index("gz") % 2)) % 4
    steps = (offsets[:, plane] + 2) // 4 % 16
    state = (19, 4, 16, 128)
    rows = (ITEMS, 4, 128)
    face = (10, 24, 128)
    phase, keep, give = call(
        first_kernel, [(4, 16, 128), rows, rows], (fluid, order), [VMEM] * 2, name="moments"
    )
    for step in range(STEPS):
        got = swap("gz", give, 0)
        (pair,) = call(pair_kernel, [(2, *rows)], (keep, got), [VMEM] * 2, name="pair")
        crossed = cross_planes(pair, steps[step])
        other = swap("gz", crossed, 0)
        stack, edge = call(
            stack_kernel,
            [(4, 32, 128), (ITEMS - 3, 8, 128)],
            (phase, crossed, other),
            [VMEM] * 3,
            name="stack",
        )
        wide, one, two = call(
            functools.partial(ghost_kernel, step),
            [(8, 32, 128), (32, 128), (32, 128)],
            (offsets, weights, stack, swap("gx", stack, 0), swap("gx", stack, 1)),
            [SMEM] * 2 + [VMEM] * 3,
            [pltpu.VMEM((12, 32, 128), F32)],
            name="ghosts",
        )
        post, east, west = call(
            collide_kernel,
            [(38, 4, 16, 128), face, face],
            (wide, one, two, swap("gz", one, 0), swap("gz", two, 1), edge, fluid, order),
            [VMEM] * 8,
            [
                pltpu.VMEM((5, 8, 128), F32),
                pltpu.VMEM((8, 32, 128), F32),
                pltpu.VMEM((10, 16, 128), F32),
                pltpu.VMEM((10, 16, 128), F32),
            ],
            name="collide",
        )
        moved, one, two = call(
            functools.partial(stream_kernel, step),
            [(38, 4, 16, 128), (16, 128), (16, 128)],
            (offsets, weights, post, east, swap("gx", east, 0), swap("gx", west, 1)),
            [SMEM] * 2 + [VMEM] * 4,
            [pltpu.VMEM((2, 12, 16, 128), F32)],
            name="stream",
        )
        more = step + 1 < STEPS
        outs = call(
            functools.partial(finish_kernel, more),
            [state, state] + ([(4, 16, 128), rows, rows] if more else []),
            (moved, swap("gz", one, 0), swap("gz", two, 1)),
            [VMEM] * 3,
            name="finish",
        )
        fluid, order = outs[:2]
        if more:
            phase, keep, give = outs[2:]
    return (fluid, order)


def solution(mesh):
    in_specs = (P(None, "gx", "gy", "gz"), P(None, "gx", "gy", "gz"), P(), P())
    out_specs = (P(None, "gx", "gy", "gz"), P(None, "gx", "gy", "gz"))
    return jax.shard_map(
        per_device, mesh=mesh, in_specs=in_specs, out_specs=out_specs, check_vma=False
    )
```

```python
import functools

import jax
import jax.numpy as jnp
from jax import lax
from jax.experimental import pallas as pl
from jax.experimental.pallas import tpu as pltpu
from jax.sharding import PartitionSpec as P

STEPS = 2

VELOCITIES = [
    (0, 0, 0),
    (1, 0, 0),
    (-1, 0, 0),
    (0, 1, 0),
    (0, -1, 0),
    (0, 0, 1),
    (0, 0, -1),
    (1, 1, 0),
    (-1, -1, 0),
    (1, -1, 0),
    (-1, 1, 0),
    (1, 0, 1),
    (-1, 0, -1),
    (1, 0, -1),
    (-1, 0, 1),
    (0, 1, 1),
    (0, -1, -1),
    (0, 1, -1),
    (0, -1, 1),
]
WEIGHTS = [1.0 / 3.0] + [1.0 / 18.0] * 6 + [1.0 / 36.0] * 12
RISING = [3, 7, 10, 15, 17]
FALLING = [4, 8, 9, 16, 18]
EAST = [i for i, c in enumerate(VELOCITIES) if c[0] == 1]
WEST = [i for i, c in enumerate(VELOCITIES) if c[0] == -1]
FRONT = [i for i, c in enumerate(VELOCITIES) if c[2] == 1]
BACK = [i for i, c in enumerate(VELOCITIES) if c[2] == -1]
A = -0.0625
B = 0.0625
K = 0.04
M = 0.5
TAU_F = 0.8
TAU_G = 0.9
U = 0.05

OWN = 8
BELOW_EDGE = 2
ABOVE_EDGE = 28
ITEMS = 17

REACH = [(k, side, (1 - 2 * side) * VELOCITIES[RISING[k % 5]][0]) for k in range(10) for side in (0, 1)]
FROM_WEST = [(k, side, place) for k, side, cx in REACH for place in range(2 - cx, 4)]
FROM_EAST = [(k, side, place) for k, side, cx in REACH for place in range(8, 10 - cx)]
GHOSTS = 160
FAR = (1, 2, 8, 9, 22, 23, 28, 29)

VMEM = pl.BlockSpec(memory_space=pltpu.VMEM)
SMEM = pl.BlockSpec(memory_space=pltpu.SMEM)
F32 = jnp.float32


def call(body, outs, operands, specs, scratch=(), name=None):
    return pl.pallas_call(
        body,
        out_shape=[jax.ShapeDtypeStruct(shape, F32) for shape in outs],
        in_specs=specs,
        out_specs=[VMEM] * len(outs),
        scratch_shapes=list(scratch),
        compiler_params=pltpu.CompilerParams(vmem_limit_bytes=32 * 1024 * 1024),
        name=name,
    )(*operands)


def lanes(shape):
    return lax.broadcasted_iota(jnp.int32, shape, 1)


def rows_of(shape):
    return lax.broadcasted_iota(jnp.int32, shape, 0)


def shift(value, amount, axis):
    amount = amount % value.shape[axis]
    return value if amount == 0 else pltpu.roll(value, amount, axis)


def plane_shift(offsets, step, plane):
    return lax.rem(offsets[step, plane] + 2, 4) - 2


def planes():
    block = lax.axis_index("gy")
    return block, lax.rem(block + 3, 4)


def is_odd(axis):
    return lax.rem(lax.axis_index(axis), 2) == 1


def swapped(odd, one, two):
    return jnp.where(odd, two, one), jnp.where(odd, one, two)


def edge_messages(fluid, order, phase_ref, keep_ref, give_ref):
    odd = is_odd("gz")

    def put(item, x, low, high):
        keep, give = swapped(odd, high, low)
        keep_ref[item, x : x + 1, :] = keep
        give_ref[item, x : x + 1, :] = give

    for x in range(4):
        f = [fluid(i, x) for i in range(19)]
        g = [order(i, x) for i in range(19)]
        phase = sum(g[1:], g[0])
        phase_ref[x] = phase
        for item in range(3):
            put(item, x, phase[item : item + 1], phase[13 + item : 14 + item])
        fields = [sum(f[1:], f[0])]
        for q in range(3):
            plus = [f[i] for i, c in enumerate(VELOCITIES) if c[q] == 1]
            minus = [f[i] for i, c in enumerate(VELOCITIES) if c[q] == -1]
            fields.append(sum(plus[1:], plus[0]) - sum(minus[1:], minus[0]))
        for n, field in enumerate(fields):
            put(3 + n, x, field[0:1], field[15:16])
        for n in range(5):
            put(7 + n, x, f[FALLING[n]][0:1], f[RISING[n]][15:16])
            put(12 + n, x, g[FALLING[n]][0:1], g[RISING[n]][15:16])


def first_kernel(f_ref, g_ref, *rest):
    edge_messages(lambda i, x: f_ref[i, x], lambda i, x: g_ref[i, x], *rest)


def pair_kernel(keep_ref, got_ref, pair_ref):
    pair_ref[0] = keep_ref[...]
    pair_ref[1] = got_ref[...]


def stack_kernel(phase_ref, crossed_ref, other_ref, stack_ref, edge_ref, send_one, send_two):
    odd = is_odd("gz")
    for x in range(4):
        stack_ref[x, 0:8, :] = jnp.zeros((8, 128), F32)
        stack_ref[x, OWN : OWN + 16, :] = phase_ref[x]
    for item in range(ITEMS):
        above, below = swapped(odd, crossed_ref[1, item], other_ref[0, item])
        if item < 3:
            for x in range(4):
                stack_ref[x, item : item + 1, :] = below[x : x + 1]
                stack_ref[x, 3 + item : 4 + item, :] = above[x : x + 1]
        else:
            edge_ref[item - 3, 0:4, :] = below
            edge_ref[item - 3, 4:8, :] = above
    odd = is_odd("gx")
    for n in range(2):
        rows = slice(24 * n, 24 * n + 24)
        send_one[rows, :], send_two[rows, :] = swapped(odd, stack_ref[3 - n], stack_ref[n])
    for n, row in enumerate(FAR):
        row = row - 25 if row >= ABOVE_EDGE else row
        at = slice(48 + n, 49 + n)
        send_one[at, :], send_two[at, :] = swapped(
            odd, stack_ref[1, row : row + 1, :], stack_ref[2, row : row + 1, :]
        )


def ghost_kernel(
    step, offsets, weights, own_ref, one_ref, two_ref, phase_ref, send_one, send_two, wide
):
    up, down = planes()
    r_down = plane_shift(offsets, step, down)
    r_up = plane_shift(offsets, step, up)
    w_down = weights[down]
    w_up = weights[up]
    odd = is_odd("gx")

    def place_cell(place, value):
        wide[place, 0:24, :] = value
        wide[place, 24:32, :] = jnp.zeros((8, 128), F32)
        wide[place, ABOVE_EDGE : ABOVE_EDGE + 3, :] = value[3:6]

    for x in range(4):
        place_cell(4 + x, own_ref[x])
    for n in range(2):
        rows = slice(24 * n, 24 * n + 24)
        east, west = swapped(odd, one_ref[rows, :], two_ref[rows, :])
        place_cell(3 - n, west)
        place_cell(8 + n, east)
    east, west = swapped(odd, one_ref[48:56, :], two_ref[48:56, :])
    for place, value in ((1, west), (10, east)):
        wide[place] = jnp.zeros((32, 128), F32)
        for n, row_number in enumerate(FAR):
            wide[place, row_number : row_number + 1, :] = value[n : n + 1]
    shape = (32, 128)
    row = rows_of(shape)
    lane = lanes(shape)
    first = jnp.zeros(shape, F32)
    last = jnp.zeros(shape, F32)

    def rise(place, r, w):
        return w * wide[place - r] + (1.0 - w) * wide[place - r - 1]

    def fall(place, r, w):
        return w * wide[place + r] + (1.0 - w) * wide[place + r + 1]

    for n in range(8):
        place = n + 2
        value = wide[place]
        if 1 <= n <= 6:
            value = jnp.where((row == 6) | (row == 7), shift(rise(place, r_down, w_down), 5, 0), value)
            value = jnp.where((row == 3) | (row == 4), shift(fall(place, r_down, w_down), -5, 0), value)
            value = jnp.where((row == 24) | (row == 25), shift(fall(place, r_up, w_up), -4, 0), value)
            value = jnp.where((row == 26) | (row == 27), shift(rise(place, r_up, w_up), 4, 0), value)
        phase_ref[n] = value
        first = jnp.where(lane // 2 == n, shift(value, 2 * n, 1), first)
        last = jnp.where(lane // 2 == n, shift(value, 2 * n - 126, 1), last)
    send_one[...], send_two[...] = swapped(is_odd("gz"), last, first)


def bulk_potential(phase, around):
    return A * phase + B * phase * phase * phase - K * (around - 6.0 * phase)


def collide_kernel(
    phase_ref,
    sent_one,
    sent_two,
    got_one,
    got_two,
    edge_ref,
    f_ref,
    g_ref,
    post_ref,
    edges_ref,
    send_one,
    send_two,
    ghost,
    pots,
    east,
    west,
):
    shape = (32, 128)
    lane = lanes(shape)
    odd = is_odd("gz")
    last, first = swapped(odd, sent_one[...], sent_two[...])
    right, left = swapped(odd, got_one[...], got_two[...])

    def updown(value):
        return shift(value, 1, 0) + shift(value, -1, 0)

    left_pot = bulk_potential(
        left, shift(left, 2, 1) + shift(left, -2, 1) + updown(left) + shift(left, 1, 1) + shift(first, 1, 1)
    )
    right_pot = bulk_potential(
        right,
        shift(right, 2, 1) + shift(right, -2, 1) + updown(right) + shift(right, -1, 1) + shift(last, -1, 1),
    )
    for n in range(1, 7):
        value = phase_ref[n]
        before = jnp.where(lane == 0, shift(left, -(2 * n + 1), 1), shift(value, 1, 1))
        after = jnp.where(lane == 127, shift(right, 127 - 2 * n, 1), shift(value, -1, 1))
        around = phase_ref[n - 1] + phase_ref[n + 1] + updown(value) + before + after
        pots[n] = bulk_potential(value, around)

    for x in range(4):
        n = x + 2
        phase_all = phase_ref[n]
        pot_all = pots[n]
        gx_all = 0.5 * (pots[n + 1] - pots[n - 1])
        gy_all = 0.5 * (shift(pot_all, -1, 0) - shift(pot_all, 1, 0))
        before = jnp.where(lane == 0, shift(left_pot, -(2 * n + 1), 1), shift(pot_all, 1, 1))
        after = jnp.where(lane == 127, shift(right_pot, 127 - 2 * n, 1), shift(pot_all, -1, 1))
        gz_all = 0.5 * (after - before)
        for k, value in enumerate((phase_all, pot_all, gx_all, gy_all, gz_all)):
            ghost[k, x : x + 1, :] = value[BELOW_EDGE : BELOW_EDGE + 1]
            ghost[k, 4 + x : 5 + x, :] = value[ABOVE_EDGE : ABOVE_EDGE + 1]
        own = slice(OWN, OWN + 16)
        phase = phase_all[own]
        pot = pot_all[own]
        grad = (gx_all[own], gy_all[own], gz_all[own])

        f = [f_ref[i, x] for i in range(19)]
        density = sum(f[1:], f[0])
        momentum = []
        for q in range(3):
            plus = [f[i] for i, c in enumerate(VELOCITIES) if c[q] == 1]
            minus = [f[i] for i, c in enumerate(VELOCITIES) if c[q] == -1]
            momentum.append(sum(plus[1:], plus[0]) - sum(minus[1:], minus[0]))
        inverse = 1.0 / density
        speed = [m * inverse for m in momentum]
        force = TAU_F * phase * inverse
        shifted = [s - force * d for s, d in zip(speed, grad)]
        square = shifted[0] * shifted[0] + shifted[1] * shifted[1] + shifted[2] * shifted[2]
        rest = 1.0 - 1.5 * square
        keep_f = 1.0 - 1.0 / TAU_F
        keep_g = 1.0 - 1.0 / TAU_G

        def store(i, fs, gs):
            post_ref[i, x] = fs
            post_ref[19 + i, x] = gs
            if x == 3 and i in EAST:
                k = EAST.index(i)
                east[k] = fs
                east[5 + k] = gs
            if x == 0 and i in WEST:
                k = WEST.index(i)
                west[k] = fs
                west[5 + k] = gs

        store(
            0,
            keep_f * f[0] + (WEIGHTS[0] / TAU_F) * density * rest,
            keep_g * g_ref[0, x] + (1.0 / TAU_G) * (phase - 2.0 * M * pot),
        )
        flow_scale = 3.0 * phase
        for i in range(1, 19, 2):
            along = directed(VELOCITIES[i], shifted)
            flow = directed(VELOCITIES[i], speed)
            scale = (WEIGHTS[i] / TAU_F) * density
            even = scale * (rest + 4.5 * along * along)
            odd = scale * (3.0 * along)
            g_even = (WEIGHTS[i] / TAU_G * 3.0 * M) * pot
            g_odd = (WEIGHTS[i] / TAU_G) * (flow_scale * flow)
            store(i, keep_f * f[i] + (even + odd), keep_g * g_ref[i, x] + (g_even + g_odd))
            store(i + 1, keep_f * f[i + 1] + (even - odd), keep_g * g_ref[i + 1, x] + (g_even - g_odd))

    sign = jnp.where(rows_of((8, 128)) < 4, 1.0, -1.0)
    phase, pot, gx, gy, gz = (ghost[k] for k in range(5))
    density = edge_ref[0]
    inverse = 1.0 / density
    speed = [edge_ref[1 + q] * inverse for q in range(3)]
    force = TAU_F * phase * inverse
    shifted = [s - force * d for s, d in zip(speed, (gx, gy, gz))]
    square = shifted[0] * shifted[0] + shifted[1] * shifted[1] + shifted[2] * shifted[2]
    rest = 1.0 - 1.5 * square
    for k, i in enumerate(RISING):
        along = sign * directed(VELOCITIES[i], shifted)
        flow = sign * directed(VELOCITIES[i], speed)
        feq = WEIGHTS[i] * density * (rest + 3.0 * along + 4.5 * along * along)
        fs = (1.0 - 1.0 / TAU_F) * edge_ref[4 + k] + (1.0 / TAU_F) * feq
        fs = fs - (3.0 * WEIGHTS[i] * VELOCITIES[i][0] * U) * density
        geq = WEIGHTS[i] * (3.0 * M * pot + 3.0 * phase * flow)
        gs = (1.0 - 1.0 / TAU_G) * edge_ref[9 + k] + (1.0 / TAU_G) * geq
        edges_ref[k] = fs
        edges_ref[5 + k] = gs
    odd = is_odd("gx")
    for k in range(10):
        rows = slice(16 * k, 16 * k + 16)
        send_one[rows, :], send_two[rows, :] = swapped(odd, east[k], west[k])
    for n, (to_east, to_west) in enumerate(zip(FROM_WEST, FROM_EAST)):
        values = []
        for k, side, place in (to_east, to_west):
            at = 4 * side + place % 4
            values.append(edges_ref[k, at : at + 1, :])
        at = slice(GHOSTS + n, GHOSTS + n + 1)
        send_one[at, :], send_two[at, :] = swapped(odd, *values)


def directed(velocity, parts):
    total = None
    for c, part in zip(velocity, parts):
        if c == 1:
            total = part if total is None else total + part
        elif c == -1:
            total = -part if total is None else total - part
    return total


def stream_kernel(
    step, offsets, weights, post_ref, own_ref, one_ref, two_ref, out_ref, send_one, send_two, wide
):
    up, down = planes()
    r_down = plane_shift(offsets, step, down)
    r_up = plane_shift(offsets, step, up)
    w_down = weights[down]
    w_up = weights[up]
    odd = is_odd("gx")
    for k in range(10):
        for side in (0, 1):
            for x in range(4):
                at = 4 * side + x
                wide[side, 4 + x, k : k + 1, :] = own_ref[k, at : at + 1, :]
    for first in range(0, len(FROM_WEST), 8):
        rows = slice(GHOSTS + first, GHOSTS + first + 8)
        from_east, from_west = swapped(odd, one_ref[rows, :], two_ref[rows, :])
        for value, table in ((from_east, FROM_EAST), (from_west, FROM_WEST)):
            for n, (k, side, place) in enumerate(table[first : first + 8]):
                wide[side, place, k : k + 1, :] = value[n : n + 1]
    shape = (16, 128)
    row = rows_of(shape)
    lane = lanes(shape)
    first = jnp.zeros(shape, F32)
    last = jnp.zeros(shape, F32)
    for x in range(4):
        place = x + 4
        risen = {}
        fallen = {}
        for c in (-1, 0, 1):
            at = place - c - r_down
            risen[c] = w_down * wide[0, at] + (1.0 - w_down) * wide[0, at - 1]
            at = place - c + r_up
            fallen[c] = w_up * wide[1, at] + (1.0 - w_up) * wide[1, at + 1]
        for i in range(38):
            part, component = divmod(i, 19)
            cx, cy, cz = VELOCITIES[component]
            source = x - cx
            if source < 0:
                k = 5 * part + EAST.index(component)
                rows = slice(16 * k, 16 * k + 16)
                value = jnp.where(odd, one_ref[rows, :], two_ref[rows, :])
            elif source > 3:
                k = 5 * part + WEST.index(component)
                rows = slice(16 * k, 16 * k + 16)
                value = jnp.where(odd, two_ref[rows, :], one_ref[rows, :])
            else:
                value = post_ref[i, source]
            if cy == 1:
                k = 5 * part + RISING.index(component)
                value = jnp.where(row == 0, risen[cx][k : k + 1], shift(value, 1, 0))
            elif cy == -1:
                k = 5 * part + FALLING.index(component)
                value = jnp.where(row == 15, fallen[cx][k : k + 1], shift(value, -1, 0))
            out_ref[i, x] = value
            if cz == 1:
                at = 4 * (5 * part + FRONT.index(component)) + x
                last = jnp.where(lane == at, shift(value, at - 127, 1), last)
            elif cz == -1:
                at = 4 * (5 * part + BACK.index(component)) + x
                first = jnp.where(lane == at, shift(value, at, 1), first)
    send_one[...], send_two[...] = swapped(is_odd("gz"), last, first)


def finish_kernel(more, moved_ref, one_ref, two_ref, f_ref, g_ref, *rest):
    lane = lanes((16, 128))
    right, left = swapped(is_odd("gz"), one_ref[...], two_ref[...])
    for x in range(4):
        for i in range(38):
            part, component = divmod(i, 19)
            value = moved_ref[i, x]
            cz = VELOCITIES[component][2]
            if cz == 1:
                at = 4 * (5 * part + FRONT.index(component)) + x
                value = jnp.where(lane == 0, shift(left, -at, 1), shift(value, 1, 1))
            elif cz == -1:
                at = 4 * (5 * part + BACK.index(component)) + x
                value = jnp.where(lane == 127, shift(right, 127 - at, 1), shift(value, -1, 1))
            (g_ref if part else f_ref)[component, x] = value
    if more:
        edge_messages(lambda i, x: f_ref[i, x], lambda i, x: g_ref[i, x], *rest)


def swap(axis, values, parity):
    count = lax.axis_size(axis)
    pairs = []
    for low in range(parity, count, 2):
        high = (low + 1) % count
        pairs += [(low, high), (high, low)]
    return lax.ppermute(values, axis, pairs)


def plane_pairs(count_x, blocks_y, count_z, steps):
    def number(x, y, z):
        return (x % count_x * blocks_y + y % blocks_y) * count_z + z

    pairs = []
    for x in range(count_x):
        for y in range(blocks_y):
            for z in range(0, count_z, 2):
                pairs.append((number(x, y, z), number(x + steps, y + 1, z + 1)))
                pairs.append((number(x + steps, y + 1, z + 1), number(x, y, z)))
    return pairs


def cross_planes(rows, steps):
    axes = ("gx", "gy", "gz")
    sizes = [lax.axis_size(axis) for axis in axes]

    def branch(number):
        pairs = plane_pairs(*sizes, number)
        return lambda sent: lax.ppermute(sent, axes, pairs)

    return lax.switch(steps, [branch(number) for number in range(sizes[0])], rows)


def per_device(fluid, order, offsets, weights):
    plane = (lax.axis_index("gy") + 3 * (lax.axis_index("gz") % 2)) % 4
    steps = (offsets[:, plane] + 2) // 4 % 16
    state = (19, 4, 16, 128)
    rows = (ITEMS, 4, 128)
    face = (GHOSTS + len(FROM_WEST), 128)
    phase, keep, give = call(
        first_kernel, [(4, 16, 128), rows, rows], (fluid, order), [VMEM] * 2, name="moments"
    )
    for step in range(STEPS):
        got = swap("gz", give, 0)
        (pair,) = call(pair_kernel, [(2, *rows)], (keep, got), [VMEM] * 2, name="pair")
        crossed = cross_planes(pair, steps[step])
        other = swap("gz", crossed, 0)
        stack, edge, one, two = call(
            stack_kernel,
            [(4, 24, 128), (ITEMS - 3, 8, 128), (56, 128), (56, 128)],
            (phase, crossed, other),
            [VMEM] * 3,
            name="stack",
        )
        wide, one, two = call(
            functools.partial(ghost_kernel, step),
            [(8, 32, 128), (32, 128), (32, 128)],
            (offsets, weights, stack, swap("gx", one, 0), swap("gx", two, 1)),
            [SMEM] * 2 + [VMEM] * 3,
            [pltpu.VMEM((12, 32, 128), F32)],
            name="ghosts",
        )
        post, edges, east, west = call(
            collide_kernel,
            [(38, 4, 16, 128), (10, 8, 128), face, face],
            (wide, one, two, swap("gz", one, 0), swap("gz", two, 1), edge, fluid, order),
            [VMEM] * 8,
            [
                pltpu.VMEM((5, 8, 128), F32),
                pltpu.VMEM((8, 32, 128), F32),
                pltpu.VMEM((10, 16, 128), F32),
                pltpu.VMEM((10, 16, 128), F32),
            ],
            name="collide",
        )
        moved, one, two = call(
            functools.partial(stream_kernel, step),
            [(38, 4, 16, 128), (16, 128), (16, 128)],
            (offsets, weights, post, edges, swap("gx", east, 0), swap("gx", west, 1)),
            [SMEM] * 2 + [VMEM] * 4,
            [pltpu.VMEM((2, 12, 16, 128), F32)],
            name="stream",
        )
        more = step + 1 < STEPS
        outs = call(
            functools.partial(finish_kernel, more),
            [state, state] + ([(4, 16, 128), rows, rows] if more else []),
            (moved, swap("gz", one, 0), swap("gz", two, 1)),
            [VMEM] * 3,
            name="finish",
        )
        fluid, order = outs[:2]
        if more:
            phase, keep, give = outs[2:]
    return (fluid, order)


def solution(mesh):
    in_specs = (P(None, "gx", "gy", "gz"), P(None, "gx", "gy", "gz"), P(), P())
    out_specs = (P(None, "gx", "gy", "gz"), P(None, "gx", "gy", "gz"))
    return jax.shard_map(
        per_device, mesh=mesh, in_specs=in_specs, out_specs=out_specs, check_vma=False
    )
```

```python
import functools

import jax
import jax.numpy as jnp
from jax import lax
from jax.experimental import pallas as pl
from jax.experimental.pallas import tpu as pltpu
from jax.sharding import PartitionSpec as P

STEPS = 2

VELOCITIES = [
    (0, 0, 0),
    (1, 0, 0),
    (-1, 0, 0),
    (0, 1, 0),
    (0, -1, 0),
    (0, 0, 1),
    (0, 0, -1),
    (1, 1, 0),
    (-1, -1, 0),
    (1, -1, 0),
    (-1, 1, 0),
    (1, 0, 1),
    (-1, 0, -1),
    (1, 0, -1),
    (-1, 0, 1),
    (0, 1, 1),
    (0, -1, -1),
    (0, 1, -1),
    (0, -1, 1),
]
WEIGHTS = [1.0 / 3.0] + [1.0 / 18.0] * 6 + [1.0 / 36.0] * 12
RISING = [3, 7, 10, 15, 17]
FALLING = [4, 8, 9, 16, 18]
EAST = [i for i, c in enumerate(VELOCITIES) if c[0] == 1]
WEST = [i for i, c in enumerate(VELOCITIES) if c[0] == -1]
FRONT = [i for i, c in enumerate(VELOCITIES) if c[2] == 1]
BACK = [i for i, c in enumerate(VELOCITIES) if c[2] == -1]
A = -0.0625
B = 0.0625
K = 0.04
M = 0.5
TAU_F = 0.8
TAU_G = 0.9
U = 0.05

OWN = 8
BELOW_EDGE = 2
ABOVE_EDGE = 28
ITEMS = 17

REACH = [(k, side, (1 - 2 * side) * VELOCITIES[RISING[k % 5]][0]) for k in range(10) for side in (0, 1)]
REACH += [(10, 0, 0), (10, 1, 0)]
FROM_WEST = [(k, side, place) for k, side, cx in REACH for place in range(2 - cx, 4)]
FROM_EAST = [(k, side, place) for k, side, cx in REACH for place in range(8, 10 - cx)]
CORNERS = 160
GHOSTS = 176
FACE_ROWS = 224
SIDES = ((5, FRONT), (4, BACK))
FAR = (1, 2, 8, 9, 22, 23, 28, 29)

VMEM = pl.BlockSpec(memory_space=pltpu.VMEM)
SMEM = pl.BlockSpec(memory_space=pltpu.SMEM)
F32 = jnp.float32


def call(body, outs, operands, specs, scratch=(), name=None):
    return pl.pallas_call(
        body,
        out_shape=[jax.ShapeDtypeStruct(shape, F32) for shape in outs],
        in_specs=specs,
        out_specs=[VMEM] * len(outs),
        scratch_shapes=list(scratch),
        compiler_params=pltpu.CompilerParams(vmem_limit_bytes=32 * 1024 * 1024),
        name=name,
    )(*operands)


def lanes(shape):
    return lax.broadcasted_iota(jnp.int32, shape, 1)


def rows_of(shape):
    return lax.broadcasted_iota(jnp.int32, shape, 0)


def shift(value, amount, axis):
    amount = amount % value.shape[axis]
    return value if amount == 0 else pltpu.roll(value, amount, axis)


def plane_shift(offsets, step, plane):
    return lax.rem(offsets[step, plane] + 2, 4) - 2


def planes():
    block = lax.axis_index("gy")
    return block, lax.rem(block + 3, 4)


def is_odd(axis):
    return lax.rem(lax.axis_index(axis), 2) == 1


def swapped(odd, one, two):
    return jnp.where(odd, two, one), jnp.where(odd, one, two)


def edge_messages(fluid, order, phase_ref, keep_ref, give_ref, first_ref, last_ref):
    odd = is_odd("gz")
    lane = lanes((16, 128))
    first = jnp.zeros((16, 128), F32)
    last = jnp.zeros((16, 128), F32)

    def put(item, x, low, high):
        keep, give = swapped(odd, high, low)
        keep_ref[item, x : x + 1, :] = keep
        give_ref[item, x : x + 1, :] = give

    for x in range(4):
        f = [fluid(i, x) for i in range(19)]
        g = [order(i, x) for i in range(19)]
        phase = sum(g[1:], g[0])
        phase_ref[x] = phase
        for item in range(3):
            put(item, x, phase[item : item + 1], phase[13 + item : 14 + item])
        density, momentum = moments(f)
        fields = [density, *momentum]
        for n, field in enumerate(fields):
            put(3 + n, x, field[0:1], field[15:16])
        for n in range(5):
            put(7 + n, x, f[FALLING[n]][0:1], f[RISING[n]][15:16])
            put(12 + n, x, g[FALLING[n]][0:1], g[RISING[n]][15:16])
        front = [f[i] for i in FRONT] + [g[i] for i in FRONT] + fields
        back = [f[i] for i in BACK] + [g[i] for i in BACK] + fields
        for n in range(14):
            at = 8 * n + 2 * x
            last = jnp.where(lane == at, shift(front[n], at - 127, 1), last)
            first = jnp.where(lane == at, shift(back[n], at, 1), first)
    first_ref[...] = first
    last_ref[...] = last


def moments(f):
    momentum = []
    for q in range(3):
        plus = [f[i] for i, c in enumerate(VELOCITIES) if c[q] == 1]
        minus = [f[i] for i, c in enumerate(VELOCITIES) if c[q] == -1]
        momentum.append(sum(plus[1:], plus[0]) - sum(minus[1:], minus[0]))
    return sum(f[1:], f[0]), momentum


def first_kernel(f_ref, g_ref, *rest):
    edge_messages(lambda i, x: f_ref[i, x], lambda i, x: g_ref[i, x], *rest)


def pair_kernel(keep_ref, got_ref, pair_ref):
    pair_ref[0] = keep_ref[...]
    pair_ref[1] = got_ref[...]


def stack_kernel(phase_ref, crossed_ref, other_ref, stack_ref, edge_ref, send_one, send_two):
    odd = is_odd("gz")
    for x in range(4):
        stack_ref[x, 0:8, :] = jnp.zeros((8, 128), F32)
        stack_ref[x, OWN : OWN + 16, :] = phase_ref[x]
    for item in range(ITEMS):
        above, below = swapped(odd, crossed_ref[1, item], other_ref[0, item])
        if item < 3:
            for x in range(4):
                stack_ref[x, item : item + 1, :] = below[x : x + 1]
                stack_ref[x, 3 + item : 4 + item, :] = above[x : x + 1]
        else:
            edge_ref[item - 3, 0:4, :] = below
            edge_ref[item - 3, 4:8, :] = above
    odd = is_odd("gx")
    for n in range(2):
        rows = slice(24 * n, 24 * n + 24)
        send_one[rows, :], send_two[rows, :] = swapped(odd, stack_ref[3 - n], stack_ref[n])
    for n, row in enumerate(FAR):
        row = row - 25 if row >= ABOVE_EDGE else row
        at = slice(48 + n, 49 + n)
        send_one[at, :], send_two[at, :] = swapped(
            odd, stack_ref[1, row : row + 1, :], stack_ref[2, row : row + 1, :]
        )


def ghost_kernel(
    step,
    offsets,
    weights,
    own_ref,
    one_ref,
    two_ref,
    edge_ref,
    first_ref,
    last_ref,
    phase_ref,
    send_one,
    send_two,
    wide,
):
    up, down = planes()
    r_down = plane_shift(offsets, step, down)
    r_up = plane_shift(offsets, step, up)
    w_down = weights[down]
    w_up = weights[up]
    odd = is_odd("gx")

    def place_cell(place, value):
        wide[place, 0:24, :] = value
        wide[place, 24:32, :] = jnp.zeros((8, 128), F32)
        wide[place, ABOVE_EDGE : ABOVE_EDGE + 3, :] = value[3:6]

    for x in range(4):
        place_cell(4 + x, own_ref[x])
    for n in range(2):
        rows = slice(24 * n, 24 * n + 24)
        east, west = swapped(odd, one_ref[rows, :], two_ref[rows, :])
        place_cell(3 - n, west)
        place_cell(8 + n, east)
    east, west = swapped(odd, one_ref[48:56, :], two_ref[48:56, :])
    for place, value in ((1, west), (10, east)):
        wide[place] = jnp.zeros((32, 128), F32)
        for n, row_number in enumerate(FAR):
            wide[place, row_number : row_number + 1, :] = value[n : n + 1]
    shape = (32, 128)
    row = rows_of(shape)
    lane = lanes(shape)
    first = jnp.zeros(shape, F32)
    last = jnp.zeros(shape, F32)

    def rise(place, r, w):
        return w * wide[place - r] + (1.0 - w) * wide[place - r - 1]

    def fall(place, r, w):
        return w * wide[place + r] + (1.0 - w) * wide[place + r + 1]

    for n in range(8):
        place = n + 2
        value = wide[place]
        if 1 <= n <= 6:
            value = jnp.where((row == 6) | (row == 7), shift(rise(place, r_down, w_down), 5, 0), value)
            value = jnp.where((row == 3) | (row == 4), shift(fall(place, r_down, w_down), -5, 0), value)
            value = jnp.where((row == 24) | (row == 25), shift(fall(place, r_up, w_up), -4, 0), value)
            value = jnp.where((row == 26) | (row == 27), shift(rise(place, r_up, w_up), 4, 0), value)
        phase_ref[n] = value
        first = jnp.where(lane // 2 == n, shift(value, 2 * n, 1), first)
        first = jnp.where(lane == 32 + 2 * n, shift(value, 30 + 2 * n, 1), first)
        last = jnp.where(lane // 2 == n, shift(value, 2 * n - 126, 1), last)
        last = jnp.where(lane == 33 + 2 * n, shift(value, 2 * n - 92, 1), last)

    shape = (8, 128)
    lane = lanes(shape)
    below = rows_of(shape) < 4
    edge_first = jnp.zeros(shape, F32)
    edge_last = jnp.zeros(shape, F32)
    for n in range(6):
        if n < 4:
            front = back = edge_ref[n]
        else:
            one, two = edge_ref[5 * n - 13], edge_ref[5 * n - 12]
            front, back = jnp.where(below, one, two), jnp.where(below, two, one)
        edge_last = jnp.where(lane == n, shift(front, n - 127, 1), edge_last)
        edge_first = jnp.where(lane == n, shift(back, n, 1), edge_first)

    odd = is_odd("gz")
    send_one[0:32, :], send_two[0:32, :] = swapped(odd, last, first)
    send_one[32:48, :], send_two[32:48, :] = swapped(odd, last_ref[...], first_ref[...])
    send_one[48:56, :], send_two[48:56, :] = swapped(odd, edge_last, edge_first)


def bulk_potential(phase, around):
    return A * phase + B * phase * phase * phase - K * (around - 6.0 * phase)


def collide_kernel(
    phase_ref,
    sent_one,
    sent_two,
    got_one,
    got_two,
    edge_ref,
    f_ref,
    g_ref,
    post_ref,
    columns_ref,
    edges_ref,
    send_one,
    send_two,
    ghost,
    pots,
    east,
    west,
):
    shape = (32, 128)
    lane = lanes(shape)
    odd = is_odd("gz")
    last, first = swapped(odd, sent_one[0:32, :], sent_two[0:32, :])
    right, left = swapped(odd, got_one[0:32, :], got_two[0:32, :])
    raw_right, raw_left = swapped(odd, got_one[32:48, :], got_two[32:48, :])
    edge_right, edge_left = swapped(odd, got_one[48:56, :], got_two[48:56, :])

    def updown(value):
        return shift(value, 1, 0) + shift(value, -1, 0)

    left_pot = bulk_potential(
        left, shift(left, 2, 1) + shift(left, -2, 1) + updown(left) + shift(left, 1, 1) + shift(first, 1, 1)
    )
    right_pot = bulk_potential(
        right,
        shift(right, 2, 1) + shift(right, -2, 1) + updown(right) + shift(right, -1, 1) + shift(last, -1, 1),
    )
    outer = shift(left, 1, 1)
    outer_left = bulk_potential(
        outer, shift(outer, 2, 1) + shift(outer, -2, 1) + updown(outer) + left + shift(left, -32, 1)
    )
    outer = shift(right, -1, 1)
    outer_right = bulk_potential(
        outer, shift(outer, 2, 1) + shift(outer, -2, 1) + updown(outer) + right + shift(right, -32, 1)
    )
    inner_left = jnp.zeros(shape, F32)
    inner_right = jnp.zeros(shape, F32)
    for n in range(1, 7):
        value = phase_ref[n]
        before = jnp.where(lane == 0, shift(left, -(2 * n + 1), 1), shift(value, 1, 1))
        after = jnp.where(lane == 127, shift(right, 127 - 2 * n, 1), shift(value, -1, 1))
        around = phase_ref[n - 1] + phase_ref[n + 1] + updown(value) + before + after
        pot = bulk_potential(value, around)
        pots[n] = pot
        inner_left = jnp.where(lane == 2 * n + 1, shift(pot, 2 * n + 1, 1), inner_left)
        inner_right = jnp.where(lane == 2 * n, shift(pot, 2 * n - 127, 1), inner_right)

    for x in range(4):
        n = x + 2
        phase_all = phase_ref[n]
        pot_all = pots[n]
        gx_all = 0.5 * (pots[n + 1] - pots[n - 1])
        gy_all = 0.5 * (shift(pot_all, -1, 0) - shift(pot_all, 1, 0))
        before = jnp.where(lane == 0, shift(left_pot, -(2 * n + 1), 1), shift(pot_all, 1, 1))
        after = jnp.where(lane == 127, shift(right_pot, 127 - 2 * n, 1), shift(pot_all, -1, 1))
        gz_all = 0.5 * (after - before)
        for k, value in enumerate((phase_all, pot_all, gx_all, gy_all, gz_all)):
            ghost[k, x : x + 1, :] = value[BELOW_EDGE : BELOW_EDGE + 1]
            ghost[k, 4 + x : 5 + x, :] = value[ABOVE_EDGE : ABOVE_EDGE + 1]
        own = slice(OWN, OWN + 16)
        phase = phase_all[own]
        pot = pot_all[own]
        grad = (gx_all[own], gy_all[own], gz_all[own])

        f = [f_ref[i, x] for i in range(19)]
        density, momentum = moments(f)
        inverse = 1.0 / density
        speed = [m * inverse for m in momentum]
        force = TAU_F * phase * inverse
        shifted = [s - force * d for s, d in zip(speed, grad)]
        square = shifted[0] * shifted[0] + shifted[1] * shifted[1] + shifted[2] * shifted[2]
        rest = 1.0 - 1.5 * square
        keep_f = 1.0 - 1.0 / TAU_F
        keep_g = 1.0 - 1.0 / TAU_G

        def store(i, fs, gs):
            post_ref[i, x] = fs
            post_ref[19 + i, x] = gs
            if x == 3 and i in EAST:
                k = EAST.index(i)
                east[k] = fs
                east[5 + k] = gs
            if x == 0 and i in WEST:
                k = WEST.index(i)
                west[k] = fs
                west[5 + k] = gs

        store(
            0,
            keep_f * f[0] + (WEIGHTS[0] / TAU_F) * density * rest,
            keep_g * g_ref[0, x] + (1.0 / TAU_G) * (phase - 2.0 * M * pot),
        )
        flow_scale = 3.0 * phase
        for i in range(1, 19, 2):
            along = directed(VELOCITIES[i], shifted)
            flow = directed(VELOCITIES[i], speed)
            scale = (WEIGHTS[i] / TAU_F) * density
            even = scale * (rest + 4.5 * along * along)
            odd = scale * (3.0 * along)
            g_even = (WEIGHTS[i] / TAU_G * 3.0 * M) * pot
            g_odd = (WEIGHTS[i] / TAU_G) * (flow_scale * flow)
            store(i, keep_f * f[i] + (even + odd), keep_g * g_ref[i, x] + (g_even + g_odd))
            store(i + 1, keep_f * f[i + 1] + (even - odd), keep_g * g_ref[i + 1, x] + (g_even - g_odd))

    sign = jnp.where(rows_of((8, 128)) < 4, 1.0, -1.0)
    flow = Flow(edge_ref[0], [edge_ref[1 + q] for q in range(3)], *(ghost[k] for k in range(5)))
    for k, i in enumerate(RISING):
        fs, gs = flow.relax(i, edge_ref[4 + k], edge_ref[9 + k], sign)
        edges_ref[k] = fs - (3.0 * WEIGHTS[i] * VELOCITIES[i][0] * U) * flow.density
        edges_ref[5 + k] = gs

    small = lanes((8, 128))
    corner = lanes((16, 128))
    corner_east = jnp.zeros((16, 128), F32)
    corner_west = jnp.zeros((16, 128), F32)
    edge_columns = jnp.zeros((8, 128), F32)
    around = ((left, left_pot, outer_left, inner_left), (right, right_pot, inner_right, outer_right))
    for side, (lane0, components) in enumerate(SIDES):
        phase, pot, before, after = around[side]
        gx = 0.5 * (shift(pot, -2, 1) - shift(pot, 2, 1))
        gy = 0.5 * (shift(pot, -1, 0) - shift(pot, 1, 0))
        gz = 0.5 * (after - before)
        fields = (phase, pot, gx, gy, gz)
        raw = (raw_left, raw_right)[side]
        raw = [shift(raw, lane0 - 8 * n, 1) for n in range(14)]
        flow = Flow(raw[10], raw[11:], *(value[OWN : OWN + 16] for value in fields))
        for k, i in enumerate(components):
            for part, value in enumerate(flow.relax(i, raw[k], raw[5 + k])):
                columns_ref[10 * side + 5 * part + k] = value
                at = 2 * side + part
                if VELOCITIES[i][0] == 1:
                    corner_east = jnp.where(corner == at, shift(value, at - 6 - lane0, 1), corner_east)
                elif VELOCITIES[i][0] == -1:
                    corner_west = jnp.where(corner == at, shift(value, at - lane0, 1), corner_west)
        for k, value in enumerate(fields):
            for x in range(4):
                at = -(2 * x + lane0)
                ghost[k, x : x + 1, :] = shift(value[0:8], at, 1)[BELOW_EDGE : BELOW_EDGE + 1]
                high = ABOVE_EDGE - 24
                ghost[k, 4 + x : 5 + x, :] = shift(value[24:32], at, 1)[high : high + 1]
        edge = (edge_left, edge_right)[side]
        edge = [shift(edge, -n, 1) for n in range(6)]
        flow = Flow(edge[0], edge[1:4], *(ghost[k] for k in range(5)))
        turn = (sign, 1.0 - 2.0 * side)
        for part, value in enumerate(flow.relax(15, edge[4], edge[5], turn=turn)):
            at = 2 * side + part
            edge_columns = jnp.where(small == at, shift(value, at, 1), edge_columns)
    edges_ref[10] = edge_columns

    odd = is_odd("gx")
    for k in range(10):
        rows = slice(16 * k, 16 * k + 16)
        send_one[rows, :], send_two[rows, :] = swapped(odd, east[k], west[k])
    rows = slice(CORNERS, CORNERS + 16)
    send_one[rows, :], send_two[rows, :] = swapped(odd, corner_east, corner_west)
    for ref in (send_one, send_two):
        ref[FACE_ROWS - 8 : FACE_ROWS, :] = jnp.zeros((8, 128), F32)
    for n, (to_east, to_west) in enumerate(zip(FROM_WEST, FROM_EAST)):
        values = []
        for k, side, place in (to_east, to_west):
            at = 4 * side + place % 4
            values.append(edges_ref[k, at : at + 1, :])
        at = slice(GHOSTS + n, GHOSTS + n + 1)
        send_one[at, :], send_two[at, :] = swapped(odd, *values)


class Flow:
    def __init__(self, density, momentum, phase, pot, gx, gy, gz):
        inverse = 1.0 / density
        self.density = density
        self.phase = phase
        self.pot = pot
        self.speed = [m * inverse for m in momentum]
        force = TAU_F * phase * inverse
        self.shifted = [s - force * d for s, d in zip(self.speed, (gx, gy, gz))]
        square = sum(part * part for part in self.shifted)
        self.rest = 1.0 - 1.5 * square

    def relax(self, i, f, g, sign=None, turn=None):
        if turn is not None:
            along, flow = (turn[0] * v[1] + turn[1] * v[2] for v in (self.shifted, self.speed))
        else:
            along, flow = (directed(VELOCITIES[i], v) for v in (self.shifted, self.speed))
        if sign is not None:
            along, flow = sign * along, sign * flow
        feq = WEIGHTS[i] * self.density * (self.rest + 3.0 * along + 4.5 * along * along)
        geq = WEIGHTS[i] * (3.0 * M * self.pot + 3.0 * self.phase * flow)
        return (
            (1.0 - 1.0 / TAU_F) * f + (1.0 / TAU_F) * feq,
            (1.0 - 1.0 / TAU_G) * g + (1.0 / TAU_G) * geq,
        )


def directed(velocity, parts):
    total = None
    for c, part in zip(velocity, parts):
        if c == 1:
            total = part if total is None else total + part
        elif c == -1:
            total = -part if total is None else total - part
    return total


def stream_kernel(
    step, more, offsets, weights, post_ref, columns_ref, own_ref, one_ref, two_ref, f_ref, g_ref, *rest
):
    *rest, wide, columns = rest
    up, down = planes()
    r_down = plane_shift(offsets, step, down)
    r_up = plane_shift(offsets, step, up)
    w_down = weights[down]
    w_up = weights[up]
    odd = is_odd("gx")
    for k in range(11):
        for side in (0, 1):
            for x in range(4):
                at = 4 * side + x
                wide[side, 4 + x, k : k + 1, :] = own_ref[k, at : at + 1, :]
    for first in range(0, len(FROM_WEST), 8):
        rows = slice(GHOSTS + first, GHOSTS + first + 8)
        from_east, from_west = swapped(odd, one_ref[rows, :], two_ref[rows, :])
        for value, table in ((from_east, FROM_EAST), (from_west, FROM_WEST)):
            for n, (k, side, place) in enumerate(table[first : first + 8]):
                wide[side, place, k : k + 1, :] = value[n : n + 1]
    shape = (16, 128)
    row = rows_of(shape)
    lane = lanes(shape)

    def rise(x, c):
        at = x + 4 - c - r_down
        return w_down * wide[0, at] + (1.0 - w_down) * wide[0, at - 1]

    def fall(x, c):
        at = x + 4 - c + r_up
        return w_up * wide[1, at] + (1.0 - w_up) * wide[1, at + 1]

    rows = slice(CORNERS, CORNERS + 16)
    corner_east, corner_west = swapped(odd, one_ref[rows, :], two_ref[rows, :])
    risen = [rise(x, 0)[10:11] for x in range(4)]
    fallen = [fall(x, 0)[10:11] for x in range(4)]
    for side, (lane0, components) in enumerate(SIDES):
        for part in (0, 1):
            source = 2 * side + part
            for k, i in enumerate(components):
                cx, cy, _ = VELOCITIES[i]
                value = columns_ref[10 * side + 5 * part + k]
                if cx:
                    at = lane0 if cx == 1 else lane0 + 6
                    corner = corner_west if cx == 1 else corner_east
                    value = jnp.where(lane == at, shift(corner, at - source, 1), shift(value, 2 * cx, 1))
                if cy:
                    value = shift(value, cy, 0)
                    edge = 0 if cy == 1 else 15
                    for x in range(4):
                        at = lane0 + 2 * x
                        ghost = shift((risen if cy == 1 else fallen)[x], at - source, 1)
                        value = jnp.where((row == edge) & (lane == at), ghost, value)
                columns[10 * side + 5 * part + k] = value

    for x in range(4):
        risen = {c: rise(x, c) for c in (-1, 0, 1)}
        fallen = {c: fall(x, c) for c in (-1, 0, 1)}
        for i in range(38):
            part, component = divmod(i, 19)
            cx, cy, cz = VELOCITIES[component]
            source = x - cx
            if source < 0:
                k = 5 * part + EAST.index(component)
                rows = slice(16 * k, 16 * k + 16)
                value = jnp.where(odd, one_ref[rows, :], two_ref[rows, :])
            elif source > 3:
                k = 5 * part + WEST.index(component)
                rows = slice(16 * k, 16 * k + 16)
                value = jnp.where(odd, two_ref[rows, :], one_ref[rows, :])
            else:
                value = post_ref[i, source]
            if cy == 1:
                k = 5 * part + RISING.index(component)
                value = jnp.where(row == 0, risen[cx][k : k + 1], shift(value, 1, 0))
            elif cy == -1:
                k = 5 * part + FALLING.index(component)
                value = jnp.where(row == 15, fallen[cx][k : k + 1], shift(value, -1, 0))
            if cz == 1:
                column = columns[5 * part + FRONT.index(component)]
                value = jnp.where(lane == 0, shift(column, -(2 * x + 5), 1), shift(value, 1, 1))
            elif cz == -1:
                column = columns[10 + 5 * part + BACK.index(component)]
                value = jnp.where(lane == 127, shift(column, 127 - (2 * x + 4), 1), shift(value, -1, 1))
            (g_ref if part else f_ref)[component, x] = value
    if more:
        edge_messages(lambda i, x: f_ref[i, x], lambda i, x: g_ref[i, x], *rest)


def swap(axis, values, parity):
    count = lax.axis_size(axis)
    pairs = []
    for low in range(parity, count, 2):
        high = (low + 1) % count
        pairs += [(low, high), (high, low)]
    return lax.ppermute(values, axis, pairs)


def plane_pairs(count_x, blocks_y, count_z, steps):
    def number(x, y, z):
        return (x % count_x * blocks_y + y % blocks_y) * count_z + z

    pairs = []
    for x in range(count_x):
        for y in range(blocks_y):
            for z in range(0, count_z, 2):
                pairs.append((number(x, y, z), number(x + steps, y + 1, z + 1)))
                pairs.append((number(x + steps, y + 1, z + 1), number(x, y, z)))
    return pairs


def cross_planes(rows, steps):
    axes = ("gx", "gy", "gz")
    sizes = [lax.axis_size(axis) for axis in axes]

    def branch(number):
        pairs = plane_pairs(*sizes, number)
        return lambda sent: lax.ppermute(sent, axes, pairs)

    return lax.switch(steps, [branch(number) for number in range(sizes[0])], rows)


def per_device(fluid, order, offsets, weights):
    plane = (lax.axis_index("gy") + 3 * (lax.axis_index("gz") % 2)) % 4
    steps = (offsets[:, plane] + 2) // 4 % 16
    state = (19, 4, 16, 128)
    rows = (ITEMS, 4, 128)
    face = (FACE_ROWS, 128)
    before = [(4, 16, 128), rows, rows, (16, 128), (16, 128)]
    phase, keep, give, first, last = call(
        first_kernel, before, (fluid, order), [VMEM] * 2, name="moments"
    )
    for step in range(STEPS):
        got = swap("gz", give, 0)
        (pair,) = call(pair_kernel, [(2, *rows)], (keep, got), [VMEM] * 2, name="pair")
        crossed = cross_planes(pair, steps[step])
        other = swap("gz", crossed, 0)
        stack, edge, one, two = call(
            stack_kernel,
            [(4, 24, 128), (ITEMS - 3, 8, 128), (56, 128), (56, 128)],
            (phase, crossed, other),
            [VMEM] * 3,
            name="stack",
        )
        wide, one, two = call(
            functools.partial(ghost_kernel, step),
            [(8, 32, 128), (56, 128), (56, 128)],
            (offsets, weights, stack, swap("gx", one, 0), swap("gx", two, 1), edge, first, last),
            [SMEM] * 2 + [VMEM] * 6,
            [pltpu.VMEM((12, 32, 128), F32)],
            name="ghosts",
        )
        post, columns, edges, east, west = call(
            collide_kernel,
            [(38, 4, 16, 128), (20, 16, 128), (11, 8, 128), face, face],
            (wide, one, two, swap("gz", one, 0), swap("gz", two, 1), edge, fluid, order),
            [VMEM] * 8,
            [
                pltpu.VMEM((5, 8, 128), F32),
                pltpu.VMEM((8, 32, 128), F32),
                pltpu.VMEM((10, 16, 128), F32),
                pltpu.VMEM((10, 16, 128), F32),
            ],
            name="collide",
        )
        more = step + 1 < STEPS
        outs = call(
            functools.partial(stream_kernel, step, more),
            [state, state] + (before if more else []),
            (offsets, weights, post, columns, edges, swap("gx", east, 0), swap("gx", west, 1)),
            [SMEM] * 2 + [VMEM] * 5,
            [pltpu.VMEM((2, 12, 16, 128), F32), pltpu.VMEM((20, 16, 128), F32)],
            name="stream",
        )
        fluid, order = outs[:2]
        if more:
            phase, keep, give, first, last = outs[2:]
    return (fluid, order)


def solution(mesh):
    in_specs = (P(None, "gx", "gy", "gz"), P(None, "gx", "gy", "gz"), P(), P())
    out_specs = (P(None, "gx", "gy", "gz"), P(None, "gx", "gy", "gz"))
    return jax.shard_map(
        per_device, mesh=mesh, in_specs=in_specs, out_specs=out_specs, check_vma=False
    )
```

```python
import functools

import jax
import jax.numpy as jnp
from jax import lax
from jax.experimental import pallas as pl
from jax.experimental.pallas import tpu as pltpu
from jax.sharding import PartitionSpec as P

STEPS = 2

VELOCITIES = [
    (0, 0, 0),
    (1, 0, 0),
    (-1, 0, 0),
    (0, 1, 0),
    (0, -1, 0),
    (0, 0, 1),
    (0, 0, -1),
    (1, 1, 0),
    (-1, -1, 0),
    (1, -1, 0),
    (-1, 1, 0),
    (1, 0, 1),
    (-1, 0, -1),
    (1, 0, -1),
    (-1, 0, 1),
    (0, 1, 1),
    (0, -1, -1),
    (0, 1, -1),
    (0, -1, 1),
]
WEIGHTS = [1.0 / 3.0] + [1.0 / 18.0] * 6 + [1.0 / 36.0] * 12
RISING = [3, 7, 10, 15, 17]
FALLING = [4, 8, 9, 16, 18]
EAST = [i for i, c in enumerate(VELOCITIES) if c[0] == 1]
WEST = [i for i, c in enumerate(VELOCITIES) if c[0] == -1]
FRONT = [i for i, c in enumerate(VELOCITIES) if c[2] == 1]
BACK = [i for i, c in enumerate(VELOCITIES) if c[2] == -1]
A = -0.0625
B = 0.0625
K = 0.04
M = 0.5
TAU_F = 0.8
TAU_G = 0.9
U = 0.05

OWN = 8
BELOW_EDGE = 2
ABOVE_EDGE = 28
ITEMS = 17

REACH = [(k, side, (1 - 2 * side) * VELOCITIES[RISING[k % 5]][0]) for k in range(10) for side in (0, 1)]
REACH += [(10, 0, 0), (10, 1, 0)]
FROM_WEST = [(k, side, place) for k, side, cx in REACH for place in range(2 - cx, 4)]
FROM_EAST = [(k, side, place) for k, side, cx in REACH for place in range(8, 10 - cx)]
CORNERS = 160
GHOSTS = 176
FACE_ROWS = 224
SIDES = ((5, FRONT), (4, BACK))
FAR = (1, 2, 8, 9, 22, 23, 28, 29)

VMEM = pl.BlockSpec(memory_space=pltpu.VMEM)
SMEM = pl.BlockSpec(memory_space=pltpu.SMEM)
ANY = pl.BlockSpec(memory_space=pl.ANY)
F32 = jnp.float32


def call(body, outs, operands, specs, scratch=(), name=None, out_spec=VMEM):
    return pl.pallas_call(
        body,
        out_shape=[jax.ShapeDtypeStruct(shape, F32) for shape in outs],
        in_specs=specs,
        out_specs=[out_spec] * len(outs),
        scratch_shapes=list(scratch),
        compiler_params=pltpu.CompilerParams(vmem_limit_bytes=32 * 1024 * 1024),
        name=name,
    )(*operands)


def lanes(shape):
    return lax.broadcasted_iota(jnp.int32, shape, 1)


def rows_of(shape):
    return lax.broadcasted_iota(jnp.int32, shape, 0)


def shift(value, amount, axis):
    amount = amount % value.shape[axis]
    return value if amount == 0 else pltpu.roll(value, amount, axis)


def plane_shift(offsets, step, plane):
    return lax.rem(offsets[step, plane] + 2, 4) - 2


def planes():
    block = lax.axis_index("gy")
    return block, lax.rem(block + 3, 4)


def is_odd(axis):
    return lax.rem(lax.axis_index(axis), 2) == 1


def swapped(odd, one, two):
    return jnp.where(odd, two, one), jnp.where(odd, one, two)


def edge_messages(fluid, order, phase_ref, keep_ref, give_ref, first_ref, last_ref):
    odd = is_odd("gz")
    lane = lanes((16, 128))
    first = jnp.zeros((16, 128), F32)
    last = jnp.zeros((16, 128), F32)

    def put(item, x, low, high):
        keep, give = swapped(odd, high, low)
        keep_ref[item, x : x + 1, :] = keep
        give_ref[item, x : x + 1, :] = give

    for x in range(4):
        f = [fluid(i, x) for i in range(19)]
        g = [order(i, x) for i in range(19)]
        phase = sum(g[1:], g[0])
        phase_ref[x] = phase
        for item in range(3):
            put(item, x, phase[item : item + 1], phase[13 + item : 14 + item])
        density, momentum = moments(f)
        fields = [density, *momentum]
        for n, field in enumerate(fields):
            put(3 + n, x, field[0:1], field[15:16])
        for n in range(5):
            put(7 + n, x, f[FALLING[n]][0:1], f[RISING[n]][15:16])
            put(12 + n, x, g[FALLING[n]][0:1], g[RISING[n]][15:16])
        front = [f[i] for i in FRONT] + [g[i] for i in FRONT] + fields
        back = [f[i] for i in BACK] + [g[i] for i in BACK] + fields
        for n in range(14):
            at = 8 * n + 2 * x
            last = jnp.where(lane == at, shift(front[n], at - 127, 1), last)
            first = jnp.where(lane == at, shift(back[n], at, 1), first)
    first_ref[...] = first
    last_ref[...] = last


def moments(f):
    momentum = []
    for q in range(3):
        plus = [f[i] for i, c in enumerate(VELOCITIES) if c[q] == 1]
        minus = [f[i] for i, c in enumerate(VELOCITIES) if c[q] == -1]
        momentum.append(sum(plus[1:], plus[0]) - sum(minus[1:], minus[0]))
    return sum(f[1:], f[0]), momentum


def first_kernel(f_ref, g_ref, *rest):
    edge_messages(lambda i, x: f_ref[i, x], lambda i, x: g_ref[i, x], *rest)


def pair_kernel(keep_ref, got_ref, pair_ref):
    pair_ref[0] = keep_ref[...]
    pair_ref[1] = got_ref[...]


def own_kernel(crossed_ref, own_ref):
    own_ref[...] = crossed_ref[1]


def stack_kernel(phase_ref, mine_ref, other_ref, stack_ref, edge_ref, send_one, send_two):
    odd = is_odd("gz")
    for x in range(4):
        stack_ref[x, 0:8, :] = jnp.zeros((8, 128), F32)
        stack_ref[x, OWN : OWN + 16, :] = phase_ref[x]
    for item in range(ITEMS):
        above, below = swapped(odd, mine_ref[item], other_ref[0, item])
        if item < 3:
            for x in range(4):
                stack_ref[x, item : item + 1, :] = below[x : x + 1]
                stack_ref[x, 3 + item : 4 + item, :] = above[x : x + 1]
        else:
            edge_ref[item - 3, 0:4, :] = below
            edge_ref[item - 3, 4:8, :] = above
    odd = is_odd("gx")
    for n in range(2):
        rows = slice(24 * n, 24 * n + 24)
        send_one[rows, :], send_two[rows, :] = swapped(odd, stack_ref[3 - n], stack_ref[n])
    for n, row in enumerate(FAR):
        row = row - 25 if row >= ABOVE_EDGE else row
        at = slice(48 + n, 49 + n)
        send_one[at, :], send_two[at, :] = swapped(
            odd, stack_ref[1, row : row + 1, :], stack_ref[2, row : row + 1, :]
        )


def ghost_kernel(
    step,
    offsets,
    weights,
    own_ref,
    one_ref,
    two_ref,
    edge_ref,
    first_ref,
    last_ref,
    phase_ref,
    send_one,
    send_two,
    wide,
):
    up, down = planes()
    r_down = plane_shift(offsets, step, down)
    r_up = plane_shift(offsets, step, up)
    w_down = weights[down]
    w_up = weights[up]
    odd = is_odd("gx")

    def place_cell(place, value):
        wide[place, 0:24, :] = value
        wide[place, 24:32, :] = jnp.zeros((8, 128), F32)
        wide[place, ABOVE_EDGE : ABOVE_EDGE + 3, :] = value[3:6]

    for x in range(4):
        place_cell(4 + x, own_ref[x])
    for n in range(2):
        rows = slice(24 * n, 24 * n + 24)
        east, west = swapped(odd, one_ref[rows, :], two_ref[rows, :])
        place_cell(3 - n, west)
        place_cell(8 + n, east)
    east, west = swapped(odd, one_ref[48:56, :], two_ref[48:56, :])
    for place, value in ((1, west), (10, east)):
        wide[place] = jnp.zeros((32, 128), F32)
        for n, row_number in enumerate(FAR):
            wide[place, row_number : row_number + 1, :] = value[n : n + 1]
    shape = (32, 128)
    row = rows_of(shape)
    lane = lanes(shape)
    first = jnp.zeros(shape, F32)
    last = jnp.zeros(shape, F32)

    def rise(place, r, w):
        return w * wide[place - r] + (1.0 - w) * wide[place - r - 1]

    def fall(place, r, w):
        return w * wide[place + r] + (1.0 - w) * wide[place + r + 1]

    for n in range(8):
        place = n + 2
        value = wide[place]
        if 1 <= n <= 6:
            value = jnp.where((row == 6) | (row == 7), shift(rise(place, r_down, w_down), 5, 0), value)
            value = jnp.where((row == 3) | (row == 4), shift(fall(place, r_down, w_down), -5, 0), value)
            value = jnp.where((row == 24) | (row == 25), shift(fall(place, r_up, w_up), -4, 0), value)
            value = jnp.where((row == 26) | (row == 27), shift(rise(place, r_up, w_up), 4, 0), value)
        phase_ref[n] = value
        first = jnp.where(lane // 2 == n, shift(value, 2 * n, 1), first)
        first = jnp.where(lane == 32 + 2 * n, shift(value, 30 + 2 * n, 1), first)
        last = jnp.where(lane // 2 == n, shift(value, 2 * n - 126, 1), last)
        last = jnp.where(lane == 33 + 2 * n, shift(value, 2 * n - 92, 1), last)

    shape = (8, 128)
    lane = lanes(shape)
    below = rows_of(shape) < 4
    edge_first = jnp.zeros(shape, F32)
    edge_last = jnp.zeros(shape, F32)
    for n in range(6):
        if n < 4:
            front = back = edge_ref[n]
        else:
            one, two = edge_ref[5 * n - 13], edge_ref[5 * n - 12]
            front, back = jnp.where(below, one, two), jnp.where(below, two, one)
        edge_last = jnp.where(lane == n, shift(front, n - 127, 1), edge_last)
        edge_first = jnp.where(lane == n, shift(back, n, 1), edge_first)

    odd = is_odd("gz")
    send_one[0:32, :], send_two[0:32, :] = swapped(odd, last, first)
    send_one[32:48, :], send_two[32:48, :] = swapped(odd, last_ref[...], first_ref[...])
    send_one[48:56, :], send_two[48:56, :] = swapped(odd, edge_last, edge_first)


def bulk_potential(phase, around):
    return A * phase + B * phase * phase * phase - K * (around - 6.0 * phase)


def collide_kernel(
    phase_ref,
    sent_one,
    sent_two,
    got_one,
    got_two,
    edge_ref,
    f_ref,
    g_ref,
    post_ref,
    columns_ref,
    edges_ref,
    send_one,
    send_two,
    ghost,
    pots,
    east,
    west,
):
    shape = (32, 128)
    lane = lanes(shape)
    odd = is_odd("gz")
    last, first = swapped(odd, sent_one[0:32, :], sent_two[0:32, :])
    right, left = swapped(odd, got_one[0:32, :], got_two[0:32, :])
    raw_right, raw_left = swapped(odd, got_one[32:48, :], got_two[32:48, :])
    edge_right, edge_left = swapped(odd, got_one[48:56, :], got_two[48:56, :])

    def updown(value):
        return shift(value, 1, 0) + shift(value, -1, 0)

    left_pot = bulk_potential(
        left, shift(left, 2, 1) + shift(left, -2, 1) + updown(left) + shift(left, 1, 1) + shift(first, 1, 1)
    )
    right_pot = bulk_potential(
        right,
        shift(right, 2, 1) + shift(right, -2, 1) + updown(right) + shift(right, -1, 1) + shift(last, -1, 1),
    )
    outer = shift(left, 1, 1)
    outer_left = bulk_potential(
        outer, shift(outer, 2, 1) + shift(outer, -2, 1) + updown(outer) + left + shift(left, -32, 1)
    )
    outer = shift(right, -1, 1)
    outer_right = bulk_potential(
        outer, shift(outer, 2, 1) + shift(outer, -2, 1) + updown(outer) + right + shift(right, -32, 1)
    )
    inner_left = jnp.zeros(shape, F32)
    inner_right = jnp.zeros(shape, F32)
    for n in range(1, 7):
        value = phase_ref[n]
        before = jnp.where(lane == 0, shift(left, -(2 * n + 1), 1), shift(value, 1, 1))
        after = jnp.where(lane == 127, shift(right, 127 - 2 * n, 1), shift(value, -1, 1))
        around = phase_ref[n - 1] + phase_ref[n + 1] + updown(value) + before + after
        pot = bulk_potential(value, around)
        pots[n] = pot
        inner_left = jnp.where(lane == 2 * n + 1, shift(pot, 2 * n + 1, 1), inner_left)
        inner_right = jnp.where(lane == 2 * n, shift(pot, 2 * n - 127, 1), inner_right)

    for x in range(4):
        n = x + 2
        phase_all = phase_ref[n]
        pot_all = pots[n]
        gx_all = 0.5 * (pots[n + 1] - pots[n - 1])
        gy_all = 0.5 * (shift(pot_all, -1, 0) - shift(pot_all, 1, 0))
        before = jnp.where(lane == 0, shift(left_pot, -(2 * n + 1), 1), shift(pot_all, 1, 1))
        after = jnp.where(lane == 127, shift(right_pot, 127 - 2 * n, 1), shift(pot_all, -1, 1))
        gz_all = 0.5 * (after - before)
        for k, value in enumerate((phase_all, pot_all, gx_all, gy_all, gz_all)):
            ghost[k, x : x + 1, :] = value[BELOW_EDGE : BELOW_EDGE + 1]
            ghost[k, 4 + x : 5 + x, :] = value[ABOVE_EDGE : ABOVE_EDGE + 1]
        own = slice(OWN, OWN + 16)
        phase = phase_all[own]
        pot = pot_all[own]
        grad = (gx_all[own], gy_all[own], gz_all[own])

        f = [f_ref[i, x] for i in range(19)]
        density, momentum = moments(f)
        inverse = 1.0 / density
        speed = [m * inverse for m in momentum]
        force = TAU_F * phase * inverse
        shifted = [s - force * d for s, d in zip(speed, grad)]
        square = shifted[0] * shifted[0] + shifted[1] * shifted[1] + shifted[2] * shifted[2]
        rest = 1.0 - 1.5 * square
        keep_f = 1.0 - 1.0 / TAU_F
        keep_g = 1.0 - 1.0 / TAU_G

        def store(i, fs, gs):
            post_ref[i, x] = fs
            post_ref[19 + i, x] = gs
            if x == 3 and i in EAST:
                k = EAST.index(i)
                east[k] = fs
                east[5 + k] = gs
            if x == 0 and i in WEST:
                k = WEST.index(i)
                west[k] = fs
                west[5 + k] = gs

        store(
            0,
            keep_f * f[0] + (WEIGHTS[0] / TAU_F) * density * rest,
            keep_g * g_ref[0, x] + (1.0 / TAU_G) * (phase - 2.0 * M * pot),
        )
        flow_scale = 3.0 * phase
        for i in range(1, 19, 2):
            along = directed(VELOCITIES[i], shifted)
            flow = directed(VELOCITIES[i], speed)
            scale = (WEIGHTS[i] / TAU_F) * density
            even = scale * (rest + 4.5 * along * along)
            odd = scale * (3.0 * along)
            g_even = (WEIGHTS[i] / TAU_G * 3.0 * M) * pot
            g_odd = (WEIGHTS[i] / TAU_G) * (flow_scale * flow)
            store(i, keep_f * f[i] + (even + odd), keep_g * g_ref[i, x] + (g_even + g_odd))
            store(i + 1, keep_f * f[i + 1] + (even - odd), keep_g * g_ref[i + 1, x] + (g_even - g_odd))

    sign = jnp.where(rows_of((8, 128)) < 4, 1.0, -1.0)
    flow = Flow(edge_ref[0], [edge_ref[1 + q] for q in range(3)], *(ghost[k] for k in range(5)))
    for k, i in enumerate(RISING):
        fs, gs = flow.relax(i, edge_ref[4 + k], edge_ref[9 + k], sign)
        edges_ref[k] = fs - (3.0 * WEIGHTS[i] * VELOCITIES[i][0] * U) * flow.density
        edges_ref[5 + k] = gs

    small = lanes((8, 128))
    corner = lanes((16, 128))
    corner_east = jnp.zeros((16, 128), F32)
    corner_west = jnp.zeros((16, 128), F32)
    edge_columns = jnp.zeros((8, 128), F32)
    around = ((left, left_pot, outer_left, inner_left), (right, right_pot, inner_right, outer_right))
    for side, (lane0, components) in enumerate(SIDES):
        phase, pot, before, after = around[side]
        gx = 0.5 * (shift(pot, -2, 1) - shift(pot, 2, 1))
        gy = 0.5 * (shift(pot, -1, 0) - shift(pot, 1, 0))
        gz = 0.5 * (after - before)
        fields = (phase, pot, gx, gy, gz)
        raw = (raw_left, raw_right)[side]
        raw = [shift(raw, lane0 - 8 * n, 1) for n in range(14)]
        flow = Flow(raw[10], raw[11:], *(value[OWN : OWN + 16] for value in fields))
        for k, i in enumerate(components):
            for part, value in enumerate(flow.relax(i, raw[k], raw[5 + k])):
                columns_ref[10 * side + 5 * part + k] = value
                at = 2 * side + part
                if VELOCITIES[i][0] == 1:
                    corner_east = jnp.where(corner == at, shift(value, at - 6 - lane0, 1), corner_east)
                elif VELOCITIES[i][0] == -1:
                    corner_west = jnp.where(corner == at, shift(value, at - lane0, 1), corner_west)
        for k, value in enumerate(fields):
            for x in range(4):
                at = -(2 * x + lane0)
                ghost[k, x : x + 1, :] = shift(value[0:8], at, 1)[BELOW_EDGE : BELOW_EDGE + 1]
                high = ABOVE_EDGE - 24
                ghost[k, 4 + x : 5 + x, :] = shift(value[24:32], at, 1)[high : high + 1]
        edge = (edge_left, edge_right)[side]
        edge = [shift(edge, -n, 1) for n in range(6)]
        flow = Flow(edge[0], edge[1:4], *(ghost[k] for k in range(5)))
        turn = (sign, 1.0 - 2.0 * side)
        for part, value in enumerate(flow.relax(15, edge[4], edge[5], turn=turn)):
            at = 2 * side + part
            edge_columns = jnp.where(small == at, shift(value, at, 1), edge_columns)
    edges_ref[10] = edge_columns

    odd = is_odd("gx")
    for k in range(10):
        rows = slice(16 * k, 16 * k + 16)
        send_one[rows, :], send_two[rows, :] = swapped(odd, east[k], west[k])
    rows = slice(CORNERS, CORNERS + 16)
    send_one[rows, :], send_two[rows, :] = swapped(odd, corner_east, corner_west)
    for ref in (send_one, send_two):
        ref[FACE_ROWS - 8 : FACE_ROWS, :] = jnp.zeros((8, 128), F32)
    for n, (to_east, to_west) in enumerate(zip(FROM_WEST, FROM_EAST)):
        values = []
        for k, side, place in (to_east, to_west):
            at = 4 * side + place % 4
            values.append(edges_ref[k, at : at + 1, :])
        at = slice(GHOSTS + n, GHOSTS + n + 1)
        send_one[at, :], send_two[at, :] = swapped(odd, *values)


class Flow:
    def __init__(self, density, momentum, phase, pot, gx, gy, gz):
        inverse = 1.0 / density
        self.density = density
        self.phase = phase
        self.pot = pot
        self.speed = [m * inverse for m in momentum]
        force = TAU_F * phase * inverse
        self.shifted = [s - force * d for s, d in zip(self.speed, (gx, gy, gz))]
        square = sum(part * part for part in self.shifted)
        self.rest = 1.0 - 1.5 * square

    def relax(self, i, f, g, sign=None, turn=None):
        if turn is not None:
            along, flow = (turn[0] * v[1] + turn[1] * v[2] for v in (self.shifted, self.speed))
        else:
            along, flow = (directed(VELOCITIES[i], v) for v in (self.shifted, self.speed))
        if sign is not None:
            along, flow = sign * along, sign * flow
        feq = WEIGHTS[i] * self.density * (self.rest + 3.0 * along + 4.5 * along * along)
        geq = WEIGHTS[i] * (3.0 * M * self.pot + 3.0 * self.phase * flow)
        return (
            (1.0 - 1.0 / TAU_F) * f + (1.0 / TAU_F) * feq,
            (1.0 - 1.0 / TAU_G) * g + (1.0 / TAU_G) * geq,
        )


def directed(velocity, parts):
    total = None
    for c, part in zip(velocity, parts):
        if c == 1:
            total = part if total is None else total + part
        elif c == -1:
            total = -part if total is None else total - part
    return total


def stream_kernel(
    step, more, offsets, weights, post_ref, columns_ref, own_ref, one_ref, two_ref, *rest
):
    if more:
        f_ref, g_ref, *rest, wide, columns = rest
    else:
        f_out, g_out, wide, columns, f_ref, g_ref, stored = rest
    copies = []
    up, down = planes()
    r_down = plane_shift(offsets, step, down)
    r_up = plane_shift(offsets, step, up)
    w_down = weights[down]
    w_up = weights[up]
    odd = is_odd("gx")
    for k in range(11):
        for side in (0, 1):
            for x in range(4):
                at = 4 * side + x
                wide[side, 4 + x, k : k + 1, :] = own_ref[k, at : at + 1, :]
    for first in range(0, len(FROM_WEST), 8):
        rows = slice(GHOSTS + first, GHOSTS + first + 8)
        from_east, from_west = swapped(odd, one_ref[rows, :], two_ref[rows, :])
        for value, table in ((from_east, FROM_EAST), (from_west, FROM_WEST)):
            for n, (k, side, place) in enumerate(table[first : first + 8]):
                wide[side, place, k : k + 1, :] = value[n : n + 1]
    shape = (16, 128)
    row = rows_of(shape)
    lane = lanes(shape)

    def rise(x, c):
        at = x + 4 - c - r_down
        return w_down * wide[0, at] + (1.0 - w_down) * wide[0, at - 1]

    def fall(x, c):
        at = x + 4 - c + r_up
        return w_up * wide[1, at] + (1.0 - w_up) * wide[1, at + 1]

    rows = slice(CORNERS, CORNERS + 16)
    corner_east, corner_west = swapped(odd, one_ref[rows, :], two_ref[rows, :])
    risen = [rise(x, 0)[10:11] for x in range(4)]
    fallen = [fall(x, 0)[10:11] for x in range(4)]
    for side, (lane0, components) in enumerate(SIDES):
        for part in (0, 1):
            source = 2 * side + part
            for k, i in enumerate(components):
                cx, cy, _ = VELOCITIES[i]
                value = columns_ref[10 * side + 5 * part + k]
                if cx:
                    at = lane0 if cx == 1 else lane0 + 6
                    corner = corner_west if cx == 1 else corner_east
                    value = jnp.where(lane == at, shift(corner, at - source, 1), shift(value, 2 * cx, 1))
                if cy:
                    value = shift(value, cy, 0)
                    edge = 0 if cy == 1 else 15
                    for x in range(4):
                        at = lane0 + 2 * x
                        ghost = shift((risen if cy == 1 else fallen)[x], at - source, 1)
                        value = jnp.where((row == edge) & (lane == at), ghost, value)
                columns[10 * side + 5 * part + k] = value

    for x in range(4):
        risen = {c: rise(x, c) for c in (-1, 0, 1)}
        fallen = {c: fall(x, c) for c in (-1, 0, 1)}
        for i in range(38):
            part, component = divmod(i, 19)
            cx, cy, cz = VELOCITIES[component]
            source = x - cx
            if source < 0:
                k = 5 * part + EAST.index(component)
                rows = slice(16 * k, 16 * k + 16)
                value = jnp.where(odd, one_ref[rows, :], two_ref[rows, :])
            elif source > 3:
                k = 5 * part + WEST.index(component)
                rows = slice(16 * k, 16 * k + 16)
                value = jnp.where(odd, two_ref[rows, :], one_ref[rows, :])
            else:
                value = post_ref[i, source]
            if cy == 1:
                k = 5 * part + RISING.index(component)
                value = jnp.where(row == 0, risen[cx][k : k + 1], shift(value, 1, 0))
            elif cy == -1:
                k = 5 * part + FALLING.index(component)
                value = jnp.where(row == 15, fallen[cx][k : k + 1], shift(value, -1, 0))
            if cz == 1:
                column = columns[5 * part + FRONT.index(component)]
                value = jnp.where(lane == 0, shift(column, -(2 * x + 5), 1), shift(value, 1, 1))
            elif cz == -1:
                column = columns[10 + 5 * part + BACK.index(component)]
                value = jnp.where(lane == 127, shift(column, 127 - (2 * x + 4), 1), shift(value, -1, 1))
            (g_ref if part else f_ref)[component, x] = value
        if not more:
            for n, (source, target) in enumerate(((f_ref, f_out), (g_ref, g_out))):
                copy = pltpu.make_async_copy(source.at[:, x], target.at[:, x], stored.at[n, x])
                copy.start()
                copies.append(copy)
    for copy in copies:
        copy.wait()
    if more:
        edge_messages(lambda i, x: f_ref[i, x], lambda i, x: g_ref[i, x], *rest)


def swap(axis, values, parity):
    count = lax.axis_size(axis)
    pairs = []
    for low in range(parity, count, 2):
        high = (low + 1) % count
        pairs += [(low, high), (high, low)]
    return lax.ppermute(values, axis, pairs)


def plane_pairs(count_x, blocks_y, count_z, steps):
    def number(x, y, z):
        return (x % count_x * blocks_y + y % blocks_y) * count_z + z

    pairs = []
    for x in range(count_x):
        for y in range(blocks_y):
            for z in range(0, count_z, 2):
                pairs.append((number(x, y, z), number(x + steps, y + 1, z + 1)))
                pairs.append((number(x + steps, y + 1, z + 1), number(x, y, z)))
    return pairs


def cross_planes(rows, steps):
    axes = ("gx", "gy", "gz")
    sizes = [lax.axis_size(axis) for axis in axes]

    def branch(number):
        pairs = plane_pairs(*sizes, number)
        return lambda sent: lax.ppermute(sent, axes, pairs)

    return lax.switch(steps, [branch(number) for number in range(sizes[0])], rows)


def per_device(fluid, order, offsets, weights):
    plane = (lax.axis_index("gy") + 3 * (lax.axis_index("gz") % 2)) % 4
    steps = (offsets[:, plane] + 2) // 4 % 16
    state = (19, 4, 16, 128)
    rows = (ITEMS, 4, 128)
    face = (FACE_ROWS, 128)
    before = [(4, 16, 128), rows, rows, (16, 128), (16, 128)]
    buffers = [pltpu.VMEM(state, F32), pltpu.VMEM(state, F32)]
    phase, keep, give, first, last = call(
        first_kernel, before, (fluid, order), [VMEM] * 2, name="moments"
    )
    for step in range(STEPS):
        got = swap("gz", give, 0)
        (pair,) = call(pair_kernel, [(2, *rows)], (keep, got), [VMEM] * 2, name="pair")
        crossed = cross_planes(pair, steps[step])
        other = swap("gz", crossed, 0)
        (mine,) = call(own_kernel, [rows], (crossed,), [VMEM], name="mine")
        stack, edge, one, two = call(
            stack_kernel,
            [(4, 24, 128), (ITEMS - 3, 8, 128), (56, 128), (56, 128)],
            (phase, mine, other),
            [VMEM] * 3,
            name="stack",
        )
        wide, one, two = call(
            functools.partial(ghost_kernel, step),
            [(8, 32, 128), (56, 128), (56, 128)],
            (offsets, weights, stack, swap("gx", one, 0), swap("gx", two, 1), edge, first, last),
            [SMEM] * 2 + [VMEM] * 6,
            [pltpu.VMEM((12, 32, 128), F32)],
            name="ghosts",
        )
        post, columns, edges, east, west = call(
            collide_kernel,
            [(38, 4, 16, 128), (20, 16, 128), (11, 8, 128), face, face],
            (wide, one, two, swap("gz", one, 0), swap("gz", two, 1), edge, fluid, order),
            [VMEM] * 8,
            [
                pltpu.VMEM((5, 8, 128), F32),
                pltpu.VMEM((8, 32, 128), F32),
                pltpu.VMEM((10, 16, 128), F32),
                pltpu.VMEM((10, 16, 128), F32),
            ],
            name="collide",
        )
        more = step + 1 < STEPS
        outs = call(
            functools.partial(stream_kernel, step, more),
            [state, state] + (before if more else []),
            (offsets, weights, post, columns, edges, swap("gx", east, 0), swap("gx", west, 1)),
            [SMEM] * 2 + [VMEM] * 5,
            [pltpu.VMEM((2, 12, 16, 128), F32), pltpu.VMEM((20, 16, 128), F32)]
            + ([] if more else [*buffers, pltpu.SemaphoreType.DMA((2, 4))]),
            name="stream",
            out_spec=VMEM if more else ANY,
        )
        fluid, order = outs[:2]
        if more:
            phase, keep, give, first, last = outs[2:]
    return (fluid, order)


def solution(mesh):
    in_specs = (P(None, "gx", "gy", "gz"), P(None, "gx", "gy", "gz"), P(), P())
    out_specs = (P(None, "gx", "gy", "gz"), P(None, "gx", "gy", "gz"))
    return jax.shard_map(
        per_device, mesh=mesh, in_specs=in_specs, out_specs=out_specs, check_vma=False
    )
```

```python
import functools

import jax
import jax.numpy as jnp
from jax import lax
from jax.experimental import pallas as pl
from jax.experimental.pallas import tpu as pltpu
from jax.sharding import PartitionSpec as P

STEPS = 2

VELOCITIES = [
    (0, 0, 0),
    (1, 0, 0),
    (-1, 0, 0),
    (0, 1, 0),
    (0, -1, 0),
    (0, 0, 1),
    (0, 0, -1),
    (1, 1, 0),
    (-1, -1, 0),
    (1, -1, 0),
    (-1, 1, 0),
    (1, 0, 1),
    (-1, 0, -1),
    (1, 0, -1),
    (-1, 0, 1),
    (0, 1, 1),
    (0, -1, -1),
    (0, 1, -1),
    (0, -1, 1),
]
WEIGHTS = [1.0 / 3.0] + [1.0 / 18.0] * 6 + [1.0 / 36.0] * 12
RISING = [3, 7, 10, 15, 17]
FALLING = [4, 8, 9, 16, 18]
EAST = [i for i, c in enumerate(VELOCITIES) if c[0] == 1]
WEST = [i for i, c in enumerate(VELOCITIES) if c[0] == -1]
FRONT = [i for i, c in enumerate(VELOCITIES) if c[2] == 1]
BACK = [i for i, c in enumerate(VELOCITIES) if c[2] == -1]
A = -0.0625
B = 0.0625
K = 0.04
M = 0.5
TAU_F = 0.8
TAU_G = 0.9
U = 0.05

OWN = 8
BELOW_EDGE = 2
ABOVE_EDGE = 28
ITEMS = 17

REACH = [(k, side, (1 - 2 * side) * VELOCITIES[RISING[k % 5]][0]) for k in range(10) for side in (0, 1)]
FROM_WEST = [(k, side, place) for k, side, cx in REACH for place in range(2 - cx, 4)]
FROM_EAST = [(k, side, place) for k, side, cx in REACH for place in range(8, 10 - cx)]
CORNERS = 160
GHOSTS = 168
FACE_ROWS = 208
EDGE_CELLS = ((0, 2, 8), (0, 3, 9), (1, 2, 8), (1, 3, 9))
SIDES = ((5, FRONT), (4, BACK))
FAR = (1, 2, 8, 9, 22, 23, 28, 29)

VMEM = pl.BlockSpec(memory_space=pltpu.VMEM)
SMEM = pl.BlockSpec(memory_space=pltpu.SMEM)
ANY = pl.BlockSpec(memory_space=pl.ANY)
F32 = jnp.float32


def call(body, outs, operands, specs, scratch=(), name=None, out_spec=VMEM):
    return pl.pallas_call(
        body,
        out_shape=[jax.ShapeDtypeStruct(shape, F32) for shape in outs],
        in_specs=specs,
        out_specs=[out_spec] * len(outs),
        scratch_shapes=list(scratch),
        compiler_params=pltpu.CompilerParams(vmem_limit_bytes=32 * 1024 * 1024),
        name=name,
    )(*operands)


def lanes(shape):
    return lax.broadcasted_iota(jnp.int32, shape, 1)


def rows_of(shape):
    return lax.broadcasted_iota(jnp.int32, shape, 0)


def shift(value, amount, axis):
    amount = amount % value.shape[axis]
    return value if amount == 0 else pltpu.roll(value, amount, axis)


def plane_shift(offsets, step, plane):
    return lax.rem(offsets[step, plane] + 2, 4) - 2


def planes():
    block = lax.axis_index("gy")
    return block, lax.rem(block + 3, 4)


def is_odd(axis):
    return lax.rem(lax.axis_index(axis), 2) == 1


def swapped(odd, one, two):
    return jnp.where(odd, two, one), jnp.where(odd, one, two)


def edge_messages(fluid, order, phase_ref, keep_ref, give_ref, first_ref, last_ref):
    odd = is_odd("gz")
    lane = lanes((16, 128))
    first = jnp.zeros((16, 128), F32)
    last = jnp.zeros((16, 128), F32)

    def put(item, x, low, high):
        keep, give = swapped(odd, high, low)
        keep_ref[item, x : x + 1, :] = keep
        give_ref[item, x : x + 1, :] = give

    for x in range(4):
        f = [fluid(i, x) for i in range(19)]
        g = [order(i, x) for i in range(19)]
        phase = sum(g[1:], g[0])
        phase_ref[x] = phase
        for item in range(3):
            put(item, x, phase[item : item + 1], phase[13 + item : 14 + item])
        density, momentum = moments(f)
        fields = [density, *momentum]
        for n, field in enumerate(fields):
            put(3 + n, x, field[0:1], field[15:16])
        for n in range(5):
            put(7 + n, x, f[FALLING[n]][0:1], f[RISING[n]][15:16])
            put(12 + n, x, g[FALLING[n]][0:1], g[RISING[n]][15:16])
        front = [f[i] for i in FRONT] + [g[i] for i in FRONT] + fields
        back = [f[i] for i in BACK] + [g[i] for i in BACK] + fields
        for n in range(14):
            at = 8 * n + 2 * x
            last = jnp.where(lane == at, shift(front[n], at - 127, 1), last)
            first = jnp.where(lane == at, shift(back[n], at, 1), first)
    first_ref[...] = first
    last_ref[...] = last


def moments(f):
    momentum = []
    for q in range(3):
        plus = [f[i] for i, c in enumerate(VELOCITIES) if c[q] == 1]
        minus = [f[i] for i, c in enumerate(VELOCITIES) if c[q] == -1]
        momentum.append(sum(plus[1:], plus[0]) - sum(minus[1:], minus[0]))
    return sum(f[1:], f[0]), momentum


def first_kernel(f_ref, g_ref, *rest):
    edge_messages(lambda i, x: f_ref[i, x], lambda i, x: g_ref[i, x], *rest)


def pair_kernel(keep_ref, got_ref, pair_ref):
    pair_ref[0] = keep_ref[...]
    pair_ref[1] = got_ref[...]


def own_kernel(crossed_ref, own_ref):
    own_ref[...] = crossed_ref[1]


def stack_kernel(phase_ref, mine_ref, other_ref, stack_ref, edge_ref, send_one, send_two):
    odd = is_odd("gz")
    for x in range(4):
        stack_ref[x, 0:8, :] = jnp.zeros((8, 128), F32)
        stack_ref[x, OWN : OWN + 16, :] = phase_ref[x]
    for item in range(ITEMS):
        above, below = swapped(odd, mine_ref[item], other_ref[0, item])
        if item < 3:
            for x in range(4):
                stack_ref[x, item : item + 1, :] = below[x : x + 1]
                stack_ref[x, 3 + item : 4 + item, :] = above[x : x + 1]
        else:
            edge_ref[item - 3, 0:4, :] = below
            edge_ref[item - 3, 4:8, :] = above
    odd = is_odd("gx")
    for n in range(2):
        rows = slice(24 * n, 24 * n + 24)
        send_one[rows, :], send_two[rows, :] = swapped(odd, stack_ref[3 - n], stack_ref[n])
    for n, row in enumerate(FAR):
        row = row - 25 if row >= ABOVE_EDGE else row
        at = slice(48 + n, 49 + n)
        send_one[at, :], send_two[at, :] = swapped(
            odd, stack_ref[1, row : row + 1, :], stack_ref[2, row : row + 1, :]
        )


def ghost_kernel(
    step,
    offsets,
    weights,
    own_ref,
    one_ref,
    two_ref,
    edge_ref,
    first_ref,
    last_ref,
    phase_ref,
    send_one,
    send_two,
    wide,
):
    up, down = planes()
    r_down = plane_shift(offsets, step, down)
    r_up = plane_shift(offsets, step, up)
    w_down = weights[down]
    w_up = weights[up]
    odd = is_odd("gx")

    def place_cell(place, value):
        wide[place, 0:24, :] = value
        wide[place, 24:32, :] = jnp.zeros((8, 128), F32)
        wide[place, ABOVE_EDGE : ABOVE_EDGE + 3, :] = value[3:6]

    for x in range(4):
        place_cell(4 + x, own_ref[x])
    for n in range(2):
        rows = slice(24 * n, 24 * n + 24)
        east, west = swapped(odd, one_ref[rows, :], two_ref[rows, :])
        place_cell(3 - n, west)
        place_cell(8 + n, east)
    east, west = swapped(odd, one_ref[48:56, :], two_ref[48:56, :])
    for place, value in ((1, west), (10, east)):
        wide[place] = jnp.zeros((32, 128), F32)
        for n, row_number in enumerate(FAR):
            wide[place, row_number : row_number + 1, :] = value[n : n + 1]
    shape = (32, 128)
    row = rows_of(shape)
    lane = lanes(shape)
    first = jnp.zeros(shape, F32)
    last = jnp.zeros(shape, F32)

    def rise(place, r, w):
        return w * wide[place - r] + (1.0 - w) * wide[place - r - 1]

    def fall(place, r, w):
        return w * wide[place + r] + (1.0 - w) * wide[place + r + 1]

    for n in range(8):
        place = n + 2
        value = wide[place]
        if 1 <= n <= 6:
            value = jnp.where((row == 6) | (row == 7), shift(rise(place, r_down, w_down), 5, 0), value)
            value = jnp.where((row == 3) | (row == 4), shift(fall(place, r_down, w_down), -5, 0), value)
            value = jnp.where((row == 24) | (row == 25), shift(fall(place, r_up, w_up), -4, 0), value)
            value = jnp.where((row == 26) | (row == 27), shift(rise(place, r_up, w_up), 4, 0), value)
        phase_ref[n] = value
        first = jnp.where(lane // 2 == n, shift(value, 2 * n, 1), first)
        first = jnp.where(lane == 32 + 2 * n, shift(value, 30 + 2 * n, 1), first)
        last = jnp.where(lane // 2 == n, shift(value, 2 * n - 126, 1), last)
        last = jnp.where(lane == 33 + 2 * n, shift(value, 2 * n - 92, 1), last)

    shape = (8, 128)
    lane = lanes(shape)
    below = rows_of(shape) < 4
    edge_first = jnp.zeros(shape, F32)
    edge_last = jnp.zeros(shape, F32)
    for n in range(6):
        if n < 4:
            front = back = edge_ref[n]
        else:
            one, two = edge_ref[5 * n - 13], edge_ref[5 * n - 12]
            front, back = jnp.where(below, one, two), jnp.where(below, two, one)
        edge_last = jnp.where(lane == n, shift(front, n - 127, 1), edge_last)
        edge_first = jnp.where(lane == n, shift(back, n, 1), edge_first)

    odd = is_odd("gz")
    send_one[0:32, :], send_two[0:32, :] = swapped(odd, last, first)
    send_one[32:48, :], send_two[32:48, :] = swapped(odd, last_ref[...], first_ref[...])
    send_one[48:56, :], send_two[48:56, :] = swapped(odd, edge_last, edge_first)


def bulk_potential(phase, around):
    return A * phase + B * phase * phase * phase - K * (around - 6.0 * phase)


def collide_kernel(
    phase_ref,
    sent_one,
    sent_two,
    got_one,
    got_two,
    edge_ref,
    f_ref,
    g_ref,
    post_ref,
    columns_ref,
    edges_ref,
    send_one,
    send_two,
    ghost,
    pots,
    east,
    west,
):
    shape = (32, 128)
    lane = lanes(shape)
    odd = is_odd("gz")
    last, first = swapped(odd, sent_one[0:32, :], sent_two[0:32, :])
    right, left = swapped(odd, got_one[0:32, :], got_two[0:32, :])
    raw_right, raw_left = swapped(odd, got_one[32:48, :], got_two[32:48, :])
    edge_right, edge_left = swapped(odd, got_one[48:56, :], got_two[48:56, :])

    def updown(value):
        return shift(value, 1, 0) + shift(value, -1, 0)

    left_pot = bulk_potential(
        left, shift(left, 2, 1) + shift(left, -2, 1) + updown(left) + shift(left, 1, 1) + shift(first, 1, 1)
    )
    right_pot = bulk_potential(
        right,
        shift(right, 2, 1) + shift(right, -2, 1) + updown(right) + shift(right, -1, 1) + shift(last, -1, 1),
    )
    outer = shift(left, 1, 1)
    outer_left = bulk_potential(
        outer, shift(outer, 2, 1) + shift(outer, -2, 1) + updown(outer) + left + shift(left, -32, 1)
    )
    outer = shift(right, -1, 1)
    outer_right = bulk_potential(
        outer, shift(outer, 2, 1) + shift(outer, -2, 1) + updown(outer) + right + shift(right, -32, 1)
    )
    inner_left = jnp.zeros(shape, F32)
    inner_right = jnp.zeros(shape, F32)
    for n in range(1, 7):
        value = phase_ref[n]
        before = jnp.where(lane == 0, shift(left, -(2 * n + 1), 1), shift(value, 1, 1))
        after = jnp.where(lane == 127, shift(right, 127 - 2 * n, 1), shift(value, -1, 1))
        around = phase_ref[n - 1] + phase_ref[n + 1] + updown(value) + before + after
        pot = bulk_potential(value, around)
        pots[n] = pot
        inner_left = jnp.where(lane == 2 * n + 1, shift(pot, 2 * n + 1, 1), inner_left)
        inner_right = jnp.where(lane == 2 * n, shift(pot, 2 * n - 127, 1), inner_right)

    for x in range(4):
        n = x + 2
        phase_all = phase_ref[n]
        pot_all = pots[n]
        gx_all = 0.5 * (pots[n + 1] - pots[n - 1])
        gy_all = 0.5 * (shift(pot_all, -1, 0) - shift(pot_all, 1, 0))
        before = jnp.where(lane == 0, shift(left_pot, -(2 * n + 1), 1), shift(pot_all, 1, 1))
        after = jnp.where(lane == 127, shift(right_pot, 127 - 2 * n, 1), shift(pot_all, -1, 1))
        gz_all = 0.5 * (after - before)
        for k, value in enumerate((phase_all, pot_all, gx_all, gy_all, gz_all)):
            ghost[k, x : x + 1, :] = value[BELOW_EDGE : BELOW_EDGE + 1]
            ghost[k, 4 + x : 5 + x, :] = value[ABOVE_EDGE : ABOVE_EDGE + 1]
        own = slice(OWN, OWN + 16)
        phase = phase_all[own]
        pot = pot_all[own]
        grad = (gx_all[own], gy_all[own], gz_all[own])

        f = [f_ref[i, x] for i in range(19)]
        density, momentum = moments(f)
        inverse = 1.0 / density
        speed = [m * inverse for m in momentum]
        force = TAU_F * phase * inverse
        shifted = [s - force * d for s, d in zip(speed, grad)]
        square = shifted[0] * shifted[0] + shifted[1] * shifted[1] + shifted[2] * shifted[2]
        rest = 1.0 - 1.5 * square
        keep_f = 1.0 - 1.0 / TAU_F
        keep_g = 1.0 - 1.0 / TAU_G

        def store(i, fs, gs):
            post_ref[i, x] = fs
            post_ref[19 + i, x] = gs
            if x == 3 and i in EAST:
                k = EAST.index(i)
                east[k] = fs
                east[5 + k] = gs
            if x == 0 and i in WEST:
                k = WEST.index(i)
                west[k] = fs
                west[5 + k] = gs

        store(
            0,
            keep_f * f[0] + (WEIGHTS[0] / TAU_F) * density * rest,
            keep_g * g_ref[0, x] + (1.0 / TAU_G) * (phase - 2.0 * M * pot),
        )
        flow_scale = 3.0 * phase
        for i in range(1, 19, 2):
            along = directed(VELOCITIES[i], shifted)
            flow = directed(VELOCITIES[i], speed)
            scale = (WEIGHTS[i] / TAU_F) * density
            even = scale * (rest + 4.5 * along * along)
            odd = scale * (3.0 * along)
            g_even = (WEIGHTS[i] / TAU_G * 3.0 * M) * pot
            g_odd = (WEIGHTS[i] / TAU_G) * (flow_scale * flow)
            store(i, keep_f * f[i] + (even + odd), keep_g * g_ref[i, x] + (g_even + g_odd))
            store(i + 1, keep_f * f[i + 1] + (even - odd), keep_g * g_ref[i + 1, x] + (g_even - g_odd))

    sign = jnp.where(rows_of((8, 128)) < 4, 1.0, -1.0)
    flow = Flow(edge_ref[0], [edge_ref[1 + q] for q in range(3)], *(ghost[k] for k in range(5)))
    for k, i in enumerate(RISING):
        fs, gs = flow.relax(i, edge_ref[4 + k], edge_ref[9 + k], sign)
        edges_ref[k] = fs - (3.0 * WEIGHTS[i] * VELOCITIES[i][0] * U) * flow.density
        edges_ref[5 + k] = gs

    small = lanes((8, 128))
    corner = lanes((16, 128))
    corner_east = jnp.zeros((16, 128), F32)
    corner_west = jnp.zeros((16, 128), F32)
    edge_columns = jnp.zeros((8, 128), F32)
    around = ((left, left_pot, outer_left, inner_left), (right, right_pot, inner_right, outer_right))
    for side, (lane0, components) in enumerate(SIDES):
        phase, pot, before, after = around[side]
        gx = 0.5 * (shift(pot, -2, 1) - shift(pot, 2, 1))
        gy = 0.5 * (shift(pot, -1, 0) - shift(pot, 1, 0))
        gz = 0.5 * (after - before)
        fields = (phase, pot, gx, gy, gz)
        raw = (raw_left, raw_right)[side]
        raw = [shift(raw, lane0 - 8 * n, 1) for n in range(14)]
        flow = Flow(raw[10], raw[11:], *(value[OWN : OWN + 16] for value in fields))
        for k, i in enumerate(components):
            for part, value in enumerate(flow.relax(i, raw[k], raw[5 + k])):
                columns_ref[10 * side + 5 * part + k] = value
                at = 2 * side + part
                if VELOCITIES[i][0] == 1:
                    corner_east = jnp.where(corner == at, shift(value, at - 6 - lane0, 1), corner_east)
                elif VELOCITIES[i][0] == -1:
                    corner_west = jnp.where(corner == at, shift(value, at - lane0, 1), corner_west)
        for k, value in enumerate(fields):
            for x in range(4):
                at = -(2 * x + lane0)
                ghost[k, x : x + 1, :] = shift(value[0:8], at, 1)[BELOW_EDGE : BELOW_EDGE + 1]
                high = ABOVE_EDGE - 24
                ghost[k, 4 + x : 5 + x, :] = shift(value[24:32], at, 1)[high : high + 1]
        edge = (edge_left, edge_right)[side]
        edge = [shift(edge, -n, 1) for n in range(6)]
        flow = Flow(edge[0], edge[1:4], *(ghost[k] for k in range(5)))
        turn = (sign, 1.0 - 2.0 * side)
        for part, value in enumerate(flow.relax(15, edge[4], edge[5], turn=turn)):
            at = 2 * side + part
            edge_columns = jnp.where(small == at, shift(value, at, 1), edge_columns)
    edges_ref[10] = edge_columns

    odd = is_odd("gx")
    for k in range(10):
        rows = slice(16 * k, 16 * k + 16)
        send_one[rows, :], send_two[rows, :] = swapped(odd, east[k], west[k])
    packed = []
    for n, corner in enumerate((corner_east, corner_west)):
        value = corner[0:8] + shift(corner[8:16], 4, 1)
        for r, (side, *places) in enumerate(EDGE_CELLS):
            at = 4 * side + places[n] % 4
            chosen = (rows_of((8, 128)) == r) & (small >= 8) & (small < 12)
            value = jnp.where(chosen, shift(edges_ref[10, at : at + 1, :], 8, 1), value)
        packed.append(value)
    rows = slice(CORNERS, CORNERS + 8)
    send_one[rows, :], send_two[rows, :] = swapped(odd, *packed)
    for n, (to_east, to_west) in enumerate(zip(FROM_WEST, FROM_EAST)):
        values = []
        for k, side, place in (to_east, to_west):
            at = 4 * side + place % 4
            values.append(edges_ref[k, at : at + 1, :])
        at = slice(GHOSTS + n, GHOSTS + n + 1)
        send_one[at, :], send_two[at, :] = swapped(odd, *values)


class Flow:
    def __init__(self, density, momentum, phase, pot, gx, gy, gz):
        inverse = 1.0 / density
        self.density = density
        self.phase = phase
        self.pot = pot
        self.speed = [m * inverse for m in momentum]
        force = TAU_F * phase * inverse
        self.shifted = [s - force * d for s, d in zip(self.speed, (gx, gy, gz))]
        square = sum(part * part for part in self.shifted)
        self.rest = 1.0 - 1.5 * square

    def relax(self, i, f, g, sign=None, turn=None):
        if turn is not None:
            along, flow = (turn[0] * v[1] + turn[1] * v[2] for v in (self.shifted, self.speed))
        else:
            along, flow = (directed(VELOCITIES[i], v) for v in (self.shifted, self.speed))
        if sign is not None:
            along, flow = sign * along, sign * flow
        feq = WEIGHTS[i] * self.density * (self.rest + 3.0 * along + 4.5 * along * along)
        geq = WEIGHTS[i] * (3.0 * M * self.pot + 3.0 * self.phase * flow)
        return (
            (1.0 - 1.0 / TAU_F) * f + (1.0 / TAU_F) * feq,
            (1.0 - 1.0 / TAU_G) * g + (1.0 / TAU_G) * geq,
        )


def directed(velocity, parts):
    total = None
    for c, part in zip(velocity, parts):
        if c == 1:
            total = part if total is None else total + part
        elif c == -1:
            total = -part if total is None else total - part
    return total


def stream_kernel(
    step, more, offsets, weights, post_ref, columns_ref, own_ref, one_ref, two_ref, *rest
):
    if more:
        f_ref, g_ref, *rest, wide, columns = rest
    else:
        f_out, g_out, wide, columns, f_ref, g_ref, stored = rest
    copies = []
    up, down = planes()
    r_down = plane_shift(offsets, step, down)
    r_up = plane_shift(offsets, step, up)
    w_down = weights[down]
    w_up = weights[up]
    odd = is_odd("gx")
    for k in range(11):
        for side in (0, 1):
            for x in range(4):
                at = 4 * side + x
                wide[side, 4 + x, k : k + 1, :] = own_ref[k, at : at + 1, :]
    for first in range(0, len(FROM_WEST), 8):
        rows = slice(GHOSTS + first, GHOSTS + first + 8)
        from_east, from_west = swapped(odd, one_ref[rows, :], two_ref[rows, :])
        for value, table in ((from_east, FROM_EAST), (from_west, FROM_WEST)):
            for n, (k, side, place) in enumerate(table[first : first + 8]):
                wide[side, place, k : k + 1, :] = value[n : n + 1]
    shape = (16, 128)
    row = rows_of(shape)
    lane = lanes(shape)

    def rise(x, c):
        at = x + 4 - c - r_down
        return w_down * wide[0, at] + (1.0 - w_down) * wide[0, at - 1]

    def fall(x, c):
        at = x + 4 - c + r_up
        return w_up * wide[1, at] + (1.0 - w_up) * wide[1, at + 1]

    rows = slice(CORNERS, CORNERS + 8)
    corners = swapped(odd, one_ref[rows, :], two_ref[rows, :])
    for r, (side, *places) in enumerate(EDGE_CELLS):
        for value, place in zip(corners, reversed(places)):
            wide[side, place, 10:11, :] = shift(value[r : r + 1], -8, 1)
    corner_east, corner_west = (
        jnp.concatenate([value, shift(value, -4, 1)], axis=0) for value in corners
    )
    risen = [rise(x, 0)[10:11] for x in range(4)]
    fallen = [fall(x, 0)[10:11] for x in range(4)]
    for side, (lane0, components) in enumerate(SIDES):
        for part in (0, 1):
            source = 2 * side + part
            for k, i in enumerate(components):
                cx, cy, _ = VELOCITIES[i]
                value = columns_ref[10 * side + 5 * part + k]
                if cx:
                    at = lane0 if cx == 1 else lane0 + 6
                    corner = corner_west if cx == 1 else corner_east
                    value = jnp.where(lane == at, shift(corner, at - source, 1), shift(value, 2 * cx, 1))
                if cy:
                    value = shift(value, cy, 0)
                    edge = 0 if cy == 1 else 15
                    for x in range(4):
                        at = lane0 + 2 * x
                        ghost = shift((risen if cy == 1 else fallen)[x], at - source, 1)
                        value = jnp.where((row == edge) & (lane == at), ghost, value)
                columns[10 * side + 5 * part + k] = value

    for x in range(4):
        risen = {c: rise(x, c) for c in (-1, 0, 1)}
        fallen = {c: fall(x, c) for c in (-1, 0, 1)}
        for i in range(38):
            part, component = divmod(i, 19)
            cx, cy, cz = VELOCITIES[component]
            source = x - cx
            if source < 0:
                k = 5 * part + EAST.index(component)
                rows = slice(16 * k, 16 * k + 16)
                value = jnp.where(odd, one_ref[rows, :], two_ref[rows, :])
            elif source > 3:
                k = 5 * part + WEST.index(component)
                rows = slice(16 * k, 16 * k + 16)
                value = jnp.where(odd, two_ref[rows, :], one_ref[rows, :])
            else:
                value = post_ref[i, source]
            if cy == 1:
                k = 5 * part + RISING.index(component)
                value = jnp.where(row == 0, risen[cx][k : k + 1], shift(value, 1, 0))
            elif cy == -1:
                k = 5 * part + FALLING.index(component)
                value = jnp.where(row == 15, fallen[cx][k : k + 1], shift(value, -1, 0))
            if cz == 1:
                column = columns[5 * part + FRONT.index(component)]
                value = jnp.where(lane == 0, shift(column, -(2 * x + 5), 1), shift(value, 1, 1))
            elif cz == -1:
                column = columns[10 + 5 * part + BACK.index(component)]
                value = jnp.where(lane == 127, shift(column, 127 - (2 * x + 4), 1), shift(value, -1, 1))
            (g_ref if part else f_ref)[component, x] = value
        if not more:
            for n, (source, target) in enumerate(((f_ref, f_out), (g_ref, g_out))):
                copy = pltpu.make_async_copy(source.at[:, x], target.at[:, x], stored.at[n, x])
                copy.start()
                copies.append(copy)
    for copy in copies:
        copy.wait()
    if more:
        edge_messages(lambda i, x: f_ref[i, x], lambda i, x: g_ref[i, x], *rest)


def swap(axis, values, parity):
    count = lax.axis_size(axis)
    pairs = []
    for low in range(parity, count, 2):
        high = (low + 1) % count
        pairs += [(low, high), (high, low)]
    return lax.ppermute(values, axis, pairs)


def plane_pairs(count_x, blocks_y, count_z, steps):
    def number(x, y, z):
        return (x % count_x * blocks_y + y % blocks_y) * count_z + z

    pairs = []
    for x in range(count_x):
        for y in range(blocks_y):
            for z in range(0, count_z, 2):
                pairs.append((number(x, y, z), number(x + steps, y + 1, z + 1)))
                pairs.append((number(x + steps, y + 1, z + 1), number(x, y, z)))
    return pairs


def cross_planes(rows, steps):
    axes = ("gx", "gy", "gz")
    sizes = [lax.axis_size(axis) for axis in axes]

    def branch(number):
        pairs = plane_pairs(*sizes, number)
        return lambda sent: lax.ppermute(sent, axes, pairs)

    return lax.switch(steps, [branch(number) for number in range(sizes[0])], rows)


def per_device(fluid, order, offsets, weights):
    plane = (lax.axis_index("gy") + 3 * (lax.axis_index("gz") % 2)) % 4
    steps = (offsets[:, plane] + 2) // 4 % 16
    state = (19, 4, 16, 128)
    rows = (ITEMS, 4, 128)
    face = (FACE_ROWS, 128)
    before = [(4, 16, 128), rows, rows, (16, 128), (16, 128)]
    buffers = [pltpu.VMEM(state, F32), pltpu.VMEM(state, F32)]
    phase, keep, give, first, last = call(
        first_kernel, before, (fluid, order), [VMEM] * 2, name="moments"
    )
    for step in range(STEPS):
        got = swap("gz", give, 0)
        (pair,) = call(pair_kernel, [(2, *rows)], (keep, got), [VMEM] * 2, name="pair")
        crossed = cross_planes(pair, steps[step])
        other = swap("gz", crossed, 0)
        (mine,) = call(own_kernel, [rows], (crossed,), [VMEM], name="mine")
        stack, edge, one, two = call(
            stack_kernel,
            [(4, 24, 128), (ITEMS - 3, 8, 128), (56, 128), (56, 128)],
            (phase, mine, other),
            [VMEM] * 3,
            name="stack",
        )
        wide, one, two = call(
            functools.partial(ghost_kernel, step),
            [(8, 32, 128), (56, 128), (56, 128)],
            (offsets, weights, stack, swap("gx", one, 0), swap("gx", two, 1), edge, first, last),
            [SMEM] * 2 + [VMEM] * 6,
            [pltpu.VMEM((12, 32, 128), F32)],
            name="ghosts",
        )
        post, columns, edges, east, west = call(
            collide_kernel,
            [(38, 4, 16, 128), (20, 16, 128), (11, 8, 128), face, face],
            (wide, one, two, swap("gz", one, 0), swap("gz", two, 1), edge, fluid, order),
            [VMEM] * 8,
            [
                pltpu.VMEM((5, 8, 128), F32),
                pltpu.VMEM((8, 32, 128), F32),
                pltpu.VMEM((10, 16, 128), F32),
                pltpu.VMEM((10, 16, 128), F32),
            ],
            name="collide",
        )
        more = step + 1 < STEPS
        outs = call(
            functools.partial(stream_kernel, step, more),
            [state, state] + (before if more else []),
            (offsets, weights, post, columns, edges, swap("gx", east, 0), swap("gx", west, 1)),
            [SMEM] * 2 + [VMEM] * 5,
            [pltpu.VMEM((2, 12, 16, 128), F32), pltpu.VMEM((20, 16, 128), F32)]
            + ([] if more else [*buffers, pltpu.SemaphoreType.DMA((2, 4))]),
            name="stream",
            out_spec=VMEM if more else ANY,
        )
        fluid, order = outs[:2]
        if more:
            phase, keep, give, first, last = outs[2:]
    return (fluid, order)


def solution(mesh):
    in_specs = (P(None, "gx", "gy", "gz"), P(None, "gx", "gy", "gz"), P(), P())
    out_specs = (P(None, "gx", "gy", "gz"), P(None, "gx", "gy", "gz"))
    return jax.shard_map(
        per_device, mesh=mesh, in_specs=in_specs, out_specs=out_specs, check_vma=False
    )
```
